128 devices in a mesh: camp: 16 (over y, z), tm: 8 (over x, core).
Axes of the slice: x: 4, y: 4, z: 4, core: 2. Of those that a mesh axis runs over, the one named last changes fastest.
Arguments:
- primal_start: float32 [32, 192, 32768], P('tm', None, 'camp'), may hold values from 0 to 2
- supply_start: float32 [32, 192], P('tm'), may hold values from 0 to 1
- reach_start: float32 [192, 32768], P(None, 'camp'), may hold values from 0 to 1
- spend_start: float32 [32, 32768], P('tm', 'camp'), may hold values from 0 to 0.05
- value: float32 [192, 32768], P(None, 'camp'), may hold values from 0.5 to 2
- share: float32 [192, 32768], P(None, 'camp'), may hold values from 0.05 to 1
- price: float32 [192, 32768], P(None, 'camp'), may hold values from 0.25 to 4
- reach_cap: float32 [192, 32768], P(None, 'camp'), may hold values from 0.5 to 4
- spend_limit: float32 [32768], P('camp'), may hold values from 768 to 3072
- supply: float32 [32, 192], P('tm'), may hold values from 4096 to 16384
- eligible: int32 [24, 32768], P(None, 'camp'), may hold values 0 or 1
- start_slot: int32 [32768], P('camp'), may hold values from 0 to 15
- active_span: int32 [32768], P('camp'), may hold values from 8 to 16
Outputs:
- primal: float32 [32, 192, 32768], P('tm', None, 'camp')
- supply_dual: float32 [32, 192], P('tm')
- reach_dual: float32 [192, 32768], P(None, 'camp')
- spend_dual: float32 [32, 32768], P('tm', 'camp')
The draws below stay inside these ranges and needn't reach their ends.
All inputs are finite; a program needn't handle non-finite values. No bound on the sum of `eligible` on one device may be relied on, other than what follows from the above.
Results may differ from the reference program's by a relative error of at most 0.0001.
Values sent between devices are 32-bit elements; how exact they have to be, the bound alone decides.
A program may use at most 64 MiB of HBM per device.

```python
import math
import jax
import jax.numpy as jnp

S = 192
SEG_BLOCK = 8
SLOTS = 32
ITERS = 2
CAMPAIGNS = 32768


def set_ends(values, rng, low, largest):
    place = [jax.random.randint(jax.random.fold_in(rng, axis), (), 0, length) for axis, length in enumerate(values.shape)]
    longest = values.shape.index(max(values.shape))
    beside = place[:longest] + [(place[longest] + 1) % values.shape[longest]] + place[longest + 1:]
    return values.at[tuple(place)].set(low).at[tuple(beside)].set(largest)


def steps_of(key, extent, split, low, top_value):
    loudness = 1.0
    for position, shards_of in split:
        heights = jax.random.uniform(jax.random.fold_in(jax.random.fold_in(key, 6), position), (shards_of,), jnp.float32, low / len(split), top_value / len(split))
        loudness = loudness * jnp.repeat(jnp.exp(heights), extent[position] // shards_of).reshape((-1,) + (1,) * (len(extent) - 1 - position))
    return loudness


def setup_inputs(seed: int = 0) -> dict:
    arg_keys = jax.random.split(jax.random.key(seed), 14)
    primal_start = jnp.clip(2.0 * jax.random.uniform(arg_keys[0], (SLOTS, S, CAMPAIGNS), jnp.float32) ** steps_of(arg_keys[0], (SLOTS, S, CAMPAIGNS), ((0, 8), (2, 16)), -0.2, 0.2), 0.0, 2.0)
    supply_start = jnp.clip(1.0 * jax.random.uniform(arg_keys[1], (SLOTS, S), jnp.float32) ** steps_of(arg_keys[1], (SLOTS, S), ((0, 8),), -0.2, 0.2), 0.0, 1.0)
    reach_start = jnp.clip(1.0 * jax.random.uniform(arg_keys[2], (S, CAMPAIGNS), jnp.float32) ** steps_of(arg_keys[2], (S, CAMPAIGNS), ((1, 16),), -0.2, 0.2), 0.0, 1.0)
    spend_start = jnp.clip(0.05 * jax.random.uniform(arg_keys[3], (SLOTS, CAMPAIGNS), jnp.float32) ** steps_of(arg_keys[3], (SLOTS, CAMPAIGNS), ((0, 8), (1, 16)), -0.2, 0.2), 0.0, 0.05)
    value = jnp.clip(jnp.exp(math.log(2.0) - 1.3862944 * jax.random.uniform(arg_keys[4], (S, CAMPAIGNS), jnp.float32) ** steps_of(arg_keys[4], (S, CAMPAIGNS), ((1, 16),), -0.2, 0.2)), 0.5, 2.0)
    share = jnp.clip(0.05 + 0.95 * jax.random.uniform(arg_keys[5], (S, CAMPAIGNS), jnp.float32) ** steps_of(arg_keys[5], (S, CAMPAIGNS), ((1, 16),), -0.2, 0.2), 0.05, 1.0)
    price = jnp.clip(jnp.exp(math.log(4.0) - 2.7725887 * jax.random.uniform(arg_keys[6], (S, CAMPAIGNS), jnp.float32) ** steps_of(arg_keys[6], (S, CAMPAIGNS), ((1, 16),), -0.2, 0.2)), 0.25, 4.0)
    reach_cap = jnp.clip(jnp.exp(math.log(4.0) - 2.0794415 * jax.random.uniform(arg_keys[7], (S, CAMPAIGNS), jnp.float32) ** steps_of(arg_keys[7], (S, CAMPAIGNS), ((1, 16),), -0.2, 0.2)), 0.5, 4.0)
    spend_limit = jnp.clip(jnp.exp(math.log(3072.0) - 1.3862944 * jax.random.uniform(arg_keys[8], (CAMPAIGNS,), jnp.float32) ** steps_of(arg_keys[8], (CAMPAIGNS,), ((0, 16),), -0.2, 0.2)), 768.0, 3072.0)
    supply = jnp.clip(4096.0 + 12288.0 * jax.random.uniform(arg_keys[9], (SLOTS, S), jnp.float32) ** steps_of(arg_keys[9], (SLOTS, S), ((0, 8),), -0.2, 0.2), 4096.0, 16384.0)
    eligible = set_ends((jax.random.randint(arg_keys[10], (S // SEG_BLOCK, CAMPAIGNS), 0, 4) < 3).astype(jnp.int32), jax.random.fold_in(arg_keys[10], 1), 0, 1)
    start_slot = set_ends(jax.random.randint(arg_keys[11], (CAMPAIGNS,), 0, SLOTS // 2), jax.random.fold_in(arg_keys[11], 1), 0, (SLOTS // 2) - 1).astype(jnp.int32)
    active_span = set_ends(jax.random.randint(arg_keys[12], (CAMPAIGNS,), SLOTS // 4, SLOTS // 2 + 1), jax.random.fold_in(arg_keys[12], 1), SLOTS // 4, (SLOTS // 2 + 1) - 1).astype(jnp.int32)
    return {"primal_start": primal_start, "supply_start": supply_start, "reach_start": reach_start, "spend_start": spend_start, "value": value, "share": share, "price": price, "reach_cap": reach_cap, "spend_limit": spend_limit, "supply": supply, "eligible": eligible, "start_slot": start_slot, "active_span": active_span}


def reference(primal_start, supply_start, reach_start, spend_start, value, share, price, reach_cap, spend_limit, supply, eligible, start_slot, active_span):
    slots = jnp.arange(SLOTS, dtype=jnp.int32)[:, None]
    begin = start_slot[None, :]
    finish = begin + active_span[None, :]
    active = ((slots >= begin) & (slots < finish)).astype(jnp.float32)
    elig = jnp.repeat(eligible.astype(jnp.float32), SEG_BLOCK, axis=0)
    allow = active[:, None, :] * elig[None]
    frac = jnp.clip((slots + 1 - begin).astype(jnp.float32) / active_span[None, :].astype(jnp.float32), 0.0, 1.0)
    cap = spend_limit[None, :] * frac
    sig_supply = 4.0 / CAMPAIGNS
    sig_reach = 1.0 / (2 * SLOTS)
    sig_spend = 1.0 / (S * SLOTS * SLOTS)
    anchor = (primal_start, supply_start, reach_start, spend_start)
    state = anchor
    for step in range(ITERS):
        keep = (step + 1.0) / (step + 2.0)
        primal, sdual, rdual, pdual = state
        zrev = jnp.flip(jnp.cumsum(jnp.flip(pdual, 0), 0), 0)
        grad = -value[None] + share[None] * sdual[:, :, None] + rdual[None] + price[None] * zrev[:, None, :]
        nxt = jnp.maximum(primal - 0.5 * grad, 0.0) * allow
        bar = 2.0 * nxt - primal
        used = jnp.sum(share[None] * bar, axis=2)
        new_s = jnp.maximum(sdual + sig_supply * (used - supply), 0.0)
        deliv = jnp.sum(bar, axis=0)
        new_r = jnp.maximum(rdual + sig_reach * (deliv - reach_cap), 0.0)
        spend = jnp.cumsum(jnp.sum(price[None] * bar, axis=1), 0)
        new_p = jnp.maximum(pdual + sig_spend * (spend - cap), 0.0)
        fresh = (nxt, new_s, new_r, new_p)
        state = tuple(keep * (2.0 * f - o) + (1.0 - keep) * a for f, o, a in zip(fresh, state, anchor))
    return state[0], state[1], state[2], state[3]
```

```python
import jax
import jax.numpy as jnp
from jax import lax
from jax.experimental import pallas as pl
from jax.experimental.pallas import tpu as pltpu
from jax.sharding import PartitionSpec as P

S = 192
SEG_BLOCK = 8
SLOTS = 32
CAMPAIGNS = 32768
MESH = pl.DeviceIdType.MESH
HIGHEST = lax.Precision.HIGHEST

NT = 4
CD = 2048
NL = CD // 128
LT = 2
NC = NL // LT
QR = S // 4
NG = 2
GL = NL // NG
GC = NC // NG
BLOCKED = -1e30

SIG_SUPPLY = 4.0 / CAMPAIGNS
SIG_REACH = 1.0 / (2 * SLOTS)
SIG_SPEND = 1.0 / (S * SLOTS * SLOTS)


def kernel(
    x0_hbm, s0_ref, r0_hbm, p0_ref, value_hbm, share_hbm, price_hbm, rcap_hbm,
    limit_ref, supply_ref, elig_ref, begin_ref, span_ref,
    x_ref, s_out, r_ref, p_out,
    x0, value, share, price, r0, rcap,
    deliv, from_sib, from_x, r1,
    pen, sb, s8, s1, used, uz, uy,
    pk0, pk1, cap, live, zeff, spent, tstart, tots,
    ld, siba_s, siba_r, rs_s, rs_r, ag_s, ag_r, sibb_s, sibb_r,
    t0_s, t0_r, tot_s, tot_r, uz_s, uz_r, uy_s, uy_r,
):
    camp = lax.axis_index("camp")
    tm = lax.axis_index("tm")
    y, z = camp // 4, camp % 4
    x, core = tm // 2, tm % 2
    sib = (camp, x * 2 + 1 - core)
    xs = [(camp, ((x + d) % 4) * 2 + core) for d in (1, 2, 3)]
    tms = [(camp, (tm + d) % 8) for d in range(1, 8)]
    zs = [(y * 4 + (z + d) % 4, tm) for d in (1, 2, 3)]
    ys = [(((y + d) % 4) * 4 + z, tm) for d in (1, 2, 3)]
    mine = pl.multiple_of(x * QR, 8)

    def send(src, dst, ssem, rsem, to):
        return pltpu.make_async_remote_copy(
            src_ref=src, dst_ref=dst, send_sem=ssem, recv_sem=rsem, device_id=to, device_id_type=MESH
        )

    loads = []

    def load(src, dst):
        cp = pltpu.make_async_copy(src, dst, ld.at[len(loads)])
        cp.start()
        loads.append(cp)

    load(value_hbm, value)
    for t in range(NT):
        load(x0_hbm.at[t], x0.at[t])
    load(share_hbm, share)
    load(price_hbm, price)
    load(r0_hbm, r0)
    load(rcap_hbm.at[pl.ds(mine, QR)], rcap)

    barrier = pltpu.get_barrier_semaphore()
    greet = tms + zs + ys
    for to in greet:
        pl.semaphore_signal(barrier, inc=1, device_id=to, device_id_type=MESH)

    def spread_supply(rows):
        s8[0:NT, :] = rows * -0.5
        table = s8[...]
        for t in range(NT):
            pick = (lax.broadcasted_iota(jnp.int32, (8, 128), 0) == t).astype(jnp.float32)
            sb[t] = lax.dot_general(
                table, pick, (((0,), (0,)), ((), ())), precision=HIGHEST, preferred_element_type=jnp.float32
            )

    s8[...] = jnp.zeros_like(s8)
    spread_supply(s0_ref[...])
    for b in range(S // SEG_BLOCK):
        pen[b] = jnp.where(elig_ref[b : b + 1, :] > 0, 0.0, BLOCKED)
    for t in range(NT):
        for lt in range(NL):
            pk0[t, lt : lt + 1, :] = p0_ref[t : t + 1, lt * 128 : (lt + 1) * 128]
    begin = begin_ref[...]
    span = span_ref[...]
    for t in range(NT):
        slot = tm * NT + t
        live[t] = ((slot >= begin) & (slot < begin + span)).astype(jnp.float32)
        frac = jnp.clip((slot + 1 - begin).astype(jnp.float32) / span.astype(jnp.float32), 0.0, 1.0)
        cap[t] = limit_ref[...] * frac
    tstart[tm] = pk0[0] + pk0[1] + pk0[2] + pk0[3]
    loads[0].wait()

    def value_body(rb, carry):
        rows = pl.ds(pl.multiple_of(rb * 8, 8), 8)
        value[rows, :] = 0.5 * value[rows, :] + pen[rb]
        return carry

    lax.fori_loop(0, S // 8, value_body, 0)

    pl.semaphore_wait(barrier, len(greet))

    cps = [
        send(tstart.at[tm], tstart.at[tm], t0_s.at[d], t0_r.at[d], tms[d]) for d in range(7)
    ]
    for cp in cps:
        cp.start()

    def masked_total(parts, later):
        total = None
        for m in range(8):
            keep = (m > tm) if later else (m < tm)
            term = jnp.where(keep, parts(m), 0.0)
            total = term if total is None else total + term
        return total

    def set_zeff(duals, later, rows):
        run = later
        for t in reversed(range(NT)):
            run = run + duals[t]
            zeff[t, rows, :] = jnp.where(live[t, rows, :] > 0.0, -0.5 * run, BLOCKED)

    for cp in cps:
        cp.wait()
    set_zeff(
        [pk0[t] for t in range(NT)],
        masked_total(lambda m: tstart[m], True),
        slice(0, NL),
    )
    for cp in loads[1:]:
        cp.wait()
    used[...] = jnp.zeros_like(used)

    def comp(it, i):
        zb = [
            [jnp.broadcast_to(zeff[t, i * LT + l : i * LT + l + 1, :], (8, 128)) for l in range(LT)]
            for t in range(NT)
        ]

        def body(rb, acc):
            rows = pl.ds(pl.multiple_of(rb * 8, 8), 8)
            acc = list(acc)
            uses = [None] * NT
            for l in range(LT):
                cols = pl.ds((i * LT + l) * 128, 128)
                sh = share[rows, cols]
                pr = price[rows, cols]
                rd = r0[rows, cols] if it == 0 else r1[i, l, rows, :]
                base = value[rows, cols] - 0.5 * rd
                total = None
                for t in range(NT):
                    old = x0[t, rows, cols] if it == 0 else x_ref[t, rows, cols]
                    new = jnp.maximum((old + base) + (sh * sb[t, rows, :] + pr * zb[t][l]), 0.0)
                    bar = (new + new) - old
                    acc[t * LT + l] = acc[t * LT + l] + pr * bar
                    use = sh * bar
                    uses[t] = use if uses[t] is None else uses[t] + use
                    total = bar if total is None else total + bar
                    if it == 0:
                        x_ref[t, rows, cols] = new
                    else:
                        x_ref[t, rows, cols] = (2.0 / 3.0) * bar + (1.0 / 3.0) * x0[t, rows, cols]
                deliv[it, i, l, rows, :] = total
            for t in range(NT):
                used[t, rows, :] = used[t, rows, :] + uses[t]
            return tuple(acc)

        zero = jnp.zeros((8, 128), jnp.float32)
        acc = lax.fori_loop(0, S // 8, body, (zero,) * (NT * LT), unroll=2)
        for t in range(NT):
            for l in range(LT):
                spent[it, t, i * LT + l : i * LT + l + 1, :] = jnp.sum(acc[t * LT + l], axis=0, keepdims=True)

    pend = {}

    def siba_start(it, i):
        cp = send(deliv.at[it, i, 1 - core], from_sib.at[it, i], siba_s.at[it, i], siba_r.at[it, i], sib)
        cp.start()
        pend["a", it, i] = cp

    def rs_start(it, i):
        pend["a", it, i].wait()
        deliv[it, i, core] = deliv[it, i, core] + from_sib[it, i]
        cps = []
        for d in (1, 2, 3):
            theirs = pl.multiple_of(((x + d) % 4) * QR, 8)
            cps.append(
                send(
                    deliv.at[it, i, core, pl.ds(theirs, QR)],
                    from_x.at[it, i, d - 1],
                    rs_s.at[it, i, d - 1],
                    rs_r.at[it, i, d - 1],
                    xs[d - 1],
                )
            )
        for cp in cps:
            cp.start()
        pend["rs", it, i] = cps

    def out_cols(i, half):
        return pl.ds(pl.multiple_of((i * LT + half) * 128, 128), 128)

    def ag_start(it, i):
        for cp in pend["rs", it, i]:
            cp.wait()
        rows = pl.ds(mine, QR)
        cols = out_cols(i, core)
        total = deliv[it, i, core, rows, :] + from_x[it, i, 0] + from_x[it, i, 1] + from_x[it, i, 2]
        start = r0[rows, cols]
        if it == 0:
            r1[i, core, rows, :] = jnp.maximum(start + SIG_REACH * (total - rcap[:, cols]), 0.0)
            piece = r1.at[i, core, rows]
        else:
            old = r1[i, core, rows, :]
            new = jnp.maximum(old + SIG_REACH * (total - rcap[:, cols]), 0.0)
            r_ref[rows, cols] = (2.0 / 3.0) * (2.0 * new - old) + (1.0 / 3.0) * start
            piece = r_ref.at[rows, cols]
        cps = [
            send(piece, piece, ag_s.at[it, i, d], ag_r.at[it, i, d], xs[d]) for d in range(3)
        ]
        for cp in cps:
            cp.start()
        pend["ag", it, i] = cps

    def sibb_start(it, i):
        for cp in pend["ag", it, i]:
            cp.wait()
        piece = r1.at[i, core] if it == 0 else r_ref.at[:, out_cols(i, core)]
        cp = send(piece, piece, sibb_s.at[it, i], sibb_r.at[it, i], sib)
        cp.start()
        pend["b", it, i] = cp

    def sibb_wait(it, i):
        pend["b", it, i].wait()

    def used_z(it):
        total = None
        for t in range(NT):
            term = lax.dot_general(
                jnp.ones((8, 128), jnp.float32), used[t], (((1,), (1,)), ((), ())),
                precision=HIGHEST, preferred_element_type=jnp.float32,
            )
            row = lax.broadcasted_iota(jnp.int32, (8, S), 0) == t
            term = jnp.where(row, term, 0.0)
            total = term if total is None else total + term
        uz[it, z] = total
        cps = [send(uz.at[it, z], uz.at[it, z], uz_s.at[it, d], uz_r.at[it, d], zs[d]) for d in range(3)]
        for cp in cps:
            cp.start()
        pend["uz", it] = cps

    def used_y(it):
        for cp in pend["uz", it]:
            cp.wait()
        uy[it, y] = uz[it, 0] + uz[it, 1] + uz[it, 2] + uz[it, 3]
        cps = [send(uy.at[it, y], uy.at[it, y], uy_s.at[it, d], uy_r.at[it, d], ys[d]) for d in range(3)]
        for cp in cps:
            cp.start()
        pend["uy", it] = cps

    def used_end(it):
        for cp in pend["uy", it]:
            cp.wait()
        total = uy[it, 0] + uy[it, 1] + uy[it, 2] + uy[it, 3]
        total = total[0:NT, :]
        if it == 0:
            new = jnp.maximum(s0_ref[...] + SIG_SUPPLY * (total - supply_ref[...]), 0.0)
            s1[...] = new
            spread_supply(new)
        else:
            old = s1[...]
            new = jnp.maximum(old + SIG_SUPPLY * (total - supply_ref[...]), 0.0)
            s_out[...] = (2.0 / 3.0) * (2.0 * new - old) + (1.0 / 3.0) * s0_ref[...]

    def share_total(e, g, value):
        tots[e, g, tm] = value
        cps = [
            send(tots.at[e, g, tm], tots.at[e, g, tm], tot_s.at[e, g, d], tot_r.at[e, g, d], tms[d])
            for d in range(7)
        ]
        for cp in cps:
            cp.start()
        pend["t", e, g] = cps

    def wait_total(e, g, later):
        for cp in pend["t", e, g]:
            cp.wait()
        return masked_total(lambda m: tots[e, g, m], later)

    def spend_1(it, g):
        rows = slice(g * GL, (g + 1) * GL)
        share_total(2 * it, g, spent[it, 0, rows] + spent[it, 1, rows] + spent[it, 2, rows] + spent[it, 3, rows])

    def spend_2(it, g):
        rows = slice(g * GL, (g + 1) * GL)
        run = wait_total(2 * it, g, False)
        fresh = []
        for t in range(NT):
            run = run + spent[it, t, rows]
            old = pk0[t, rows] if it == 0 else pk1[t, rows]
            new = jnp.maximum(old + SIG_SPEND * (run - cap[t, rows]), 0.0)
            if it == 0:
                pk1[t, rows] = new
                fresh.append(new)
            else:
                res = (2.0 / 3.0) * (2.0 * new - old) + (1.0 / 3.0) * pk0[t, rows]
                for lt in range(GL):
                    c = (g * GL + lt) * 128
                    p_out[t : t + 1, c : c + 128] = res[lt : lt + 1, :]
        if it == 0:
            share_total(1, g, fresh[0] + fresh[1] + fresh[2] + fresh[3])

    def spend_3(g):
        rows = slice(g * GL, (g + 1) * GL)
        later = wait_total(1, g, True)
        set_zeff([pk1[t, rows] for t in range(NT)], later, rows)

    for i in range(NC):
        comp(0, i)
        siba_start(0, i)
        if i >= 1:
            rs_start(0, i - 1)
        if i == GC - 1:
            spend_1(0, 0)
    used_z(0)
    spend_1(0, 1)
    rs_start(0, NC - 1)
    for i in range(0, 2):
        ag_start(0, i)
    spend_2(0, 0)
    for i in range(2, 4):
        ag_start(0, i)
    used_y(0)
    spend_2(0, 1)
    for i in range(4, 6):
        ag_start(0, i)
    sibb_start(0, 0)
    spend_3(0)
    ag_start(0, 6)
    sibb_start(0, 1)
    used_end(0)
    used[...] = jnp.zeros_like(used)
    ag_start(0, 7)
    for i in range(NC):
        sibb_wait(0, i)
        if i + 2 < NC:
            sibb_start(0, i + 2)
        if i == GC:
            spend_3(1)
        comp(1, i)
        siba_start(1, i)
        if i >= 1:
            rs_start(1, i - 1)
        if i >= 4:
            ag_start(1, i - 4)
        if i == GC - 1:
            spend_1(1, 0)
    used_z(1)
    spend_1(1, 1)
    rs_start(1, NC - 1)
    sibb_start(1, 0)
    ag_start(1, 4)
    sibb_start(1, 1)
    ag_start(1, 5)
    sibb_start(1, 2)
    used_y(1)
    spend_2(1, 0)
    ag_start(1, 6)
    sibb_start(1, 3)
    spend_2(1, 1)
    ag_start(1, 7)
    sibb_start(1, 4)
    used_end(1)
    for i in range(5, NC):
        sibb_start(1, i)
    for i in range(NC):
        sibb_wait(1, i)


def shards(
    primal_start, supply_start, reach_start, spend_start, value, share, price, reach_cap,
    spend_limit, supply, eligible, start_slot, active_span,
):
    f32 = jnp.float32
    vmem = pl.BlockSpec(memory_space=pltpu.VMEM)
    anywhere = pl.BlockSpec(memory_space=pltpu.HBM)
    dma = pltpu.SemaphoreType.DMA
    outs = (
        pltpu.VMEM((NT, S, CD), f32),
        jax.ShapeDtypeStruct((NT, S), f32),
        pltpu.VMEM((S, CD), f32),
        jax.ShapeDtypeStruct((NT, CD), f32),
    )
    scratch = [
        pltpu.VMEM((NT, S, CD), f32),
        pltpu.VMEM((S, CD), f32),
        pltpu.VMEM((S, CD), f32),
        pltpu.VMEM((S, CD), f32),
        pltpu.VMEM((S, CD), f32),
        pltpu.VMEM((QR, CD), f32),
        pltpu.VMEM((2, NC, LT, S, 128), f32),
        pltpu.VMEM((2, NC, S, 128), f32),
        pltpu.VMEM((2, NC, 3, QR, 128), f32),
        pltpu.VMEM((NC, LT, S, 128), f32),
        pltpu.VMEM((S // SEG_BLOCK, 1, CD), f32),
        pltpu.VMEM((NT, S, 128), f32),
        pltpu.VMEM((8, S), f32),
        pltpu.VMEM((NT, S), f32),
        pltpu.VMEM((NT, S, 128), f32),
        pltpu.VMEM((2, 4, 8, S), f32),
        pltpu.VMEM((2, 4, 8, S), f32),
        pltpu.VMEM((NT, NL, 128), f32),
        pltpu.VMEM((NT, NL, 128), f32),
        pltpu.VMEM((NT, NL, 128), f32),
        pltpu.VMEM((NT, NL, 128), f32),
        pltpu.VMEM((NT, NL, 128), f32),
        pltpu.VMEM((2, NT, NL, 128), f32),
        pltpu.VMEM((8, NL, 128), f32),
        pltpu.VMEM((3, NG, 8, GL, 128), f32),
        dma((NT + 5,)),
        dma((2, NC)), dma((2, NC)),
        dma((2, NC, 3)), dma((2, NC, 3)),
        dma((2, NC, 3)), dma((2, NC, 3)),
        dma((2, NC)), dma((2, NC)),
        dma((7,)), dma((7,)),
        dma((3, NG, 7)), dma((3, NG, 7)),
        dma((2, 3)), dma((2, 3)),
        dma((2, 3)), dma((2, 3)),
    ]
    res = pl.pallas_call(
        kernel,
        out_shape=outs,
        in_specs=[anywhere, vmem, anywhere, vmem] + [anywhere] * 4 + [vmem] * 5,
        out_specs=(vmem, vmem, vmem, vmem),
        scratch_shapes=scratch,
        compiler_params=pltpu.CompilerParams(
            collective_id=0, has_side_effects=True, vmem_limit_bytes=44 * 2**20
        ),
    )(
        primal_start, supply_start, reach_start, spend_start, value, share, price, reach_cap,
        spend_limit.reshape(NL, 128), supply, eligible,
        start_slot.reshape(NL, 128), active_span.reshape(NL, 128),
    )
    return tuple(res)


def solution(mesh):
    in_specs = (
        P("tm", None, "camp"), P("tm", None), P(None, "camp"), P("tm", "camp"),
        P(None, "camp"), P(None, "camp"), P(None, "camp"), P(None, "camp"),
        P("camp"), P("tm", None), P(None, "camp"), P("camp"), P("camp"),
    )
    out_specs = (P("tm", None, "camp"), P("tm", None), P(None, "camp"), P("tm", "camp"))
    return jax.shard_map(shards, mesh=mesh, in_specs=in_specs, out_specs=out_specs, check_vma=False)
```

```python
import jax
import jax.numpy as jnp
from jax import lax
from jax.experimental import pallas as pl
from jax.experimental.pallas import tpu as pltpu
from jax.sharding import PartitionSpec as P

S = 192
SEG_BLOCK = 8
SLOTS = 32
CAMPAIGNS = 32768
MESH = pl.DeviceIdType.MESH
HIGHEST = lax.Precision.HIGHEST

NT = 4
CD = 2048
NL = CD // 128
LT = 2
NC = NL // LT
QR = S // 4
NG = 2
GL = NL // NG
GC = NC // NG
BLOCKED = -1e30

SIG_SUPPLY = 4.0 / CAMPAIGNS
SIG_REACH = 1.0 / (2 * SLOTS)
SIG_SPEND = 1.0 / (S * SLOTS * SLOTS)


def kernel(
    x0_hbm, s0_hbm, r0_hbm, p0_hbm, value_hbm, share_hbm, price_hbm, rcap_hbm,
    limit_hbm, supply_hbm, elig_hbm, begin_hbm, span_hbm,
    x_ref, s_out, r_ref, p_out,
    s0_ref, p0_ref, limit_ref, supply_ref, elig_ref, begin_ref, span_ref,
    x0, value, share, price, r0, rcap,
    deliv, from_sib, from_x, r1,
    pen, sb, s8, s1, used, uz, uy,
    pk0, pk1, cap, live, zeff, spent, tstart, tots,
    ld, siba_s, siba_r, rs_s, rs_r, ag_s, ag_r, sibb_s, sibb_r,
    t0_s, t0_r, tot_s, tot_r, uz_s, uz_r, uy_s, uy_r,
):
    camp = lax.axis_index("camp")
    tm = lax.axis_index("tm")
    y, z = camp // 4, camp % 4
    x, core = tm // 2, tm % 2
    sib = (camp, x * 2 + 1 - core)
    xs = [(camp, ((x + d) % 4) * 2 + core) for d in (1, 2, 3)]
    tms = [(camp, (tm + d) % 8) for d in range(1, 8)]
    zs = [(y * 4 + (z + d) % 4, tm) for d in (1, 2, 3)]
    ys = [(((y + d) % 4) * 4 + z, tm) for d in (1, 2, 3)]
    mine = pl.multiple_of(x * QR, 8)

    def send(src, dst, ssem, rsem, to):
        return pltpu.make_async_remote_copy(
            src_ref=src, dst_ref=dst, send_sem=ssem, recv_sem=rsem, device_id=to, device_id_type=MESH
        )

    loads = []

    def load(src, dst):
        cp = pltpu.make_async_copy(src, dst, ld.at[len(loads)])
        cp.start()
        loads.append(cp)

    for src, dst in (
        (p0_hbm, p0_ref), (s0_hbm, s0_ref), (elig_hbm, elig_ref), (begin_hbm, begin_ref),
        (span_hbm, span_ref), (limit_hbm, limit_ref), (supply_hbm, supply_ref),
    ):
        load(src, dst)
    small = len(loads)
    load(value_hbm, value)
    for t in range(NT):
        load(x0_hbm.at[t], x0.at[t])
    load(share_hbm, share)
    load(price_hbm, price)
    load(r0_hbm, r0)
    load(rcap_hbm.at[pl.ds(mine, QR)], rcap)

    barrier = pltpu.get_barrier_semaphore()
    greet = tms + zs + ys
    for to in greet:
        pl.semaphore_signal(barrier, inc=1, device_id=to, device_id_type=MESH)

    for cp in loads[:small]:
        cp.wait()

    def spread_supply(rows):
        s8[0:NT, :] = rows * -0.5
        table = s8[...]
        for t in range(NT):
            pick = (lax.broadcasted_iota(jnp.int32, (8, 128), 0) == t).astype(jnp.float32)
            sb[t] = lax.dot_general(
                table, pick, (((0,), (0,)), ((), ())), precision=HIGHEST, preferred_element_type=jnp.float32
            )

    s8[...] = jnp.zeros_like(s8)
    spread_supply(s0_ref[...])
    for b in range(S // SEG_BLOCK):
        pen[b] = jnp.where(elig_ref[b : b + 1, :] > 0, 0.0, BLOCKED)
    for t in range(NT):
        for lt in range(NL):
            pk0[t, lt : lt + 1, :] = p0_ref[t : t + 1, lt * 128 : (lt + 1) * 128]
    begin = begin_ref[...]
    span = span_ref[...]
    for t in range(NT):
        slot = tm * NT + t
        live[t] = ((slot >= begin) & (slot < begin + span)).astype(jnp.float32)
        frac = jnp.clip((slot + 1 - begin).astype(jnp.float32) / span.astype(jnp.float32), 0.0, 1.0)
        cap[t] = limit_ref[...] * frac
    tstart[tm] = pk0[0] + pk0[1] + pk0[2] + pk0[3]
    loads[small].wait()

    def value_body(rb, carry):
        rows = pl.ds(pl.multiple_of(rb * 8, 8), 8)
        value[rows, :] = 0.5 * value[rows, :] + pen[rb]
        return carry

    lax.fori_loop(0, S // 8, value_body, 0)

    pl.semaphore_wait(barrier, len(greet))

    cps = [
        send(tstart.at[tm], tstart.at[tm], t0_s.at[d], t0_r.at[d], tms[d]) for d in range(7)
    ]
    for cp in cps:
        cp.start()

    def masked_total(parts, later):
        total = None
        for m in range(8):
            keep = (m > tm) if later else (m < tm)
            term = jnp.where(keep, parts(m), 0.0)
            total = term if total is None else total + term
        return total

    def set_zeff(duals, later, rows):
        run = later
        for t in reversed(range(NT)):
            run = run + duals[t]
            zeff[t, rows, :] = jnp.where(live[t, rows, :] > 0.0, -0.5 * run, BLOCKED)

    for cp in cps:
        cp.wait()
    set_zeff(
        [pk0[t] for t in range(NT)],
        masked_total(lambda m: tstart[m], True),
        slice(0, NL),
    )
    for cp in loads[small + 1 :]:
        cp.wait()
    used[...] = jnp.zeros_like(used)

    def comp(it, i):
        zb = [
            [jnp.broadcast_to(zeff[t, i * LT + l : i * LT + l + 1, :], (8, 128)) for l in range(LT)]
            for t in range(NT)
        ]

        def body(rb, acc):
            rows = pl.ds(pl.multiple_of(rb * 8, 8), 8)
            acc = list(acc)
            uses = [None] * NT
            for l in range(LT):
                cols = pl.ds((i * LT + l) * 128, 128)
                sh = share[rows, cols]
                pr = price[rows, cols]
                rd = r0[rows, cols] if it == 0 else r1[i, l, rows, :]
                base = value[rows, cols] - 0.5 * rd
                total = None
                for t in range(NT):
                    old = x0[t, rows, cols] if it == 0 else x_ref[t, rows, cols]
                    new = jnp.maximum((old + base) + (sh * sb[t, rows, :] + pr * zb[t][l]), 0.0)
                    bar = (new + new) - old
                    acc[t * LT + l] = acc[t * LT + l] + pr * bar
                    use = sh * bar
                    uses[t] = use if uses[t] is None else uses[t] + use
                    total = bar if total is None else total + bar
                    if it == 0:
                        x_ref[t, rows, cols] = new
                    else:
                        x_ref[t, rows, cols] = (2.0 / 3.0) * bar + (1.0 / 3.0) * x0[t, rows, cols]
                deliv[it, i, l, rows, :] = total
            for t in range(NT):
                used[t, rows, :] = used[t, rows, :] + uses[t]
            return tuple(acc)

        zero = jnp.zeros((8, 128), jnp.float32)
        acc = lax.fori_loop(0, S // 8, body, (zero,) * (NT * LT), unroll=2)
        for t in range(NT):
            for l in range(LT):
                spent[it, t, i * LT + l : i * LT + l + 1, :] = jnp.sum(acc[t * LT + l], axis=0, keepdims=True)

    pend = {}

    def siba_start(it, i):
        cp = send(deliv.at[it, i, 1 - core], from_sib.at[it, i], siba_s.at[it, i], siba_r.at[it, i], sib)
        cp.start()
        pend["a", it, i] = cp

    def rs_start(it, i):
        pend["a", it, i].wait()
        deliv[it, i, core] = deliv[it, i, core] + from_sib[it, i]
        cps = []
        for d in (1, 2, 3):
            theirs = pl.multiple_of(((x + d) % 4) * QR, 8)
            cps.append(
                send(
                    deliv.at[it, i, core, pl.ds(theirs, QR)],
                    from_x.at[it, i, d - 1],
                    rs_s.at[it, i, d - 1],
                    rs_r.at[it, i, d - 1],
                    xs[d - 1],
                )
            )
        for cp in cps:
            cp.start()
        pend["rs", it, i] = cps

    def out_cols(i, half):
        return pl.ds(pl.multiple_of((i * LT + half) * 128, 128), 128)

    def ag_start(it, i):
        for cp in pend["rs", it, i]:
            cp.wait()
        rows = pl.ds(mine, QR)
        cols = out_cols(i, core)
        total = deliv[it, i, core, rows, :] + from_x[it, i, 0] + from_x[it, i, 1] + from_x[it, i, 2]
        start = r0[rows, cols]
        if it == 0:
            r1[i, core, rows, :] = jnp.maximum(start + SIG_REACH * (total - rcap[:, cols]), 0.0)
            piece = r1.at[i, core, rows]
        else:
            old = r1[i, core, rows, :]
            new = jnp.maximum(old + SIG_REACH * (total - rcap[:, cols]), 0.0)
            r_ref[rows, cols] = (2.0 / 3.0) * (2.0 * new - old) + (1.0 / 3.0) * start
            piece = r_ref.at[rows, cols]
        cps = [
            send(piece, piece, ag_s.at[it, i, d], ag_r.at[it, i, d], xs[d]) for d in range(3)
        ]
        for cp in cps:
            cp.start()
        pend["ag", it, i] = cps

    def sibb_start(it, i):
        for cp in pend["ag", it, i]:
            cp.wait()
        piece = r1.at[i, core] if it == 0 else r_ref.at[:, out_cols(i, core)]
        cp = send(piece, piece, sibb_s.at[it, i], sibb_r.at[it, i], sib)
        cp.start()
        pend["b", it, i] = cp

    def sibb_wait(it, i):
        pend["b", it, i].wait()

    def used_z(it):
        total = None
        for t in range(NT):
            term = lax.dot_general(
                jnp.ones((8, 128), jnp.float32), used[t], (((1,), (1,)), ((), ())),
                precision=HIGHEST, preferred_element_type=jnp.float32,
            )
            row = lax.broadcasted_iota(jnp.int32, (8, S), 0) == t
            term = jnp.where(row, term, 0.0)
            total = term if total is None else total + term
        uz[it, z] = total
        cps = [send(uz.at[it, z], uz.at[it, z], uz_s.at[it, d], uz_r.at[it, d], zs[d]) for d in range(3)]
        for cp in cps:
            cp.start()
        pend["uz", it] = cps

    def used_y(it):
        for cp in pend["uz", it]:
            cp.wait()
        uy[it, y] = uz[it, 0] + uz[it, 1] + uz[it, 2] + uz[it, 3]
        cps = [send(uy.at[it, y], uy.at[it, y], uy_s.at[it, d], uy_r.at[it, d], ys[d]) for d in range(3)]
        for cp in cps:
            cp.start()
        pend["uy", it] = cps

    def used_end(it):
        for cp in pend["uy", it]:
            cp.wait()
        total = uy[it, 0] + uy[it, 1] + uy[it, 2] + uy[it, 3]
        total = total[0:NT, :]
        if it == 0:
            new = jnp.maximum(s0_ref[...] + SIG_SUPPLY * (total - supply_ref[...]), 0.0)
            s1[...] = new
            spread_supply(new)
        else:
            old = s1[...]
            new = jnp.maximum(old + SIG_SUPPLY * (total - supply_ref[...]), 0.0)
            s_out[...] = (2.0 / 3.0) * (2.0 * new - old) + (1.0 / 3.0) * s0_ref[...]

    def share_total(e, g, value):
        tots[e, g, tm] = value
        cps = [
            send(tots.at[e, g, tm], tots.at[e, g, tm], tot_s.at[e, g, d], tot_r.at[e, g, d], tms[d])
            for d in range(7)
        ]
        for cp in cps:
            cp.start()
        pend["t", e, g] = cps

    def wait_total(e, g, later):
        for cp in pend["t", e, g]:
            cp.wait()
        return masked_total(lambda m: tots[e, g, m], later)

    def spend_1(it, g):
        rows = slice(g * GL, (g + 1) * GL)
        share_total(2 * it, g, spent[it, 0, rows] + spent[it, 1, rows] + spent[it, 2, rows] + spent[it, 3, rows])

    def spend_2(it, g):
        rows = slice(g * GL, (g + 1) * GL)
        run = wait_total(2 * it, g, False)
        fresh = []
        for t in range(NT):
            run = run + spent[it, t, rows]
            old = pk0[t, rows] if it == 0 else pk1[t, rows]
            new = jnp.maximum(old + SIG_SPEND * (run - cap[t, rows]), 0.0)
            if it == 0:
                pk1[t, rows] = new
                fresh.append(new)
            else:
                res = (2.0 / 3.0) * (2.0 * new - old) + (1.0 / 3.0) * pk0[t, rows]
                for lt in range(GL):
                    c = (g * GL + lt) * 128
                    p_out[t : t + 1, c : c + 128] = res[lt : lt + 1, :]
        if it == 0:
            share_total(1, g, fresh[0] + fresh[1] + fresh[2] + fresh[3])

    def spend_3(g):
        rows = slice(g * GL, (g + 1) * GL)
        later = wait_total(1, g, True)
        set_zeff([pk1[t, rows] for t in range(NT)], later, rows)

    for i in range(NC):
        comp(0, i)
        siba_start(0, i)
        if i >= 1:
            rs_start(0, i - 1)
        if i == GC - 1:
            spend_1(0, 0)
    used_z(0)
    spend_1(0, 1)
    rs_start(0, NC - 1)
    for i in range(0, 2):
        ag_start(0, i)
    spend_2(0, 0)
    for i in range(2, 4):
        ag_start(0, i)
    used_y(0)
    spend_2(0, 1)
    for i in range(4, 6):
        ag_start(0, i)
    sibb_start(0, 0)
    spend_3(0)
    ag_start(0, 6)
    sibb_start(0, 1)
    used_end(0)
    used[...] = jnp.zeros_like(used)
    ag_start(0, 7)
    for i in range(NC):
        sibb_wait(0, i)
        if i + 2 < NC:
            sibb_start(0, i + 2)
        if i == GC:
            spend_3(1)
        comp(1, i)
        siba_start(1, i)
        if i >= 1:
            rs_start(1, i - 1)
        if i >= 4:
            ag_start(1, i - 4)
        if i == GC - 1:
            spend_1(1, 0)
    used_z(1)
    spend_1(1, 1)
    rs_start(1, NC - 1)
    sibb_start(1, 0)
    ag_start(1, 4)
    sibb_start(1, 1)
    ag_start(1, 5)
    sibb_start(1, 2)
    used_y(1)
    spend_2(1, 0)
    ag_start(1, 6)
    sibb_start(1, 3)
    spend_2(1, 1)
    ag_start(1, 7)
    sibb_start(1, 4)
    used_end(1)
    for i in range(5, NC):
        sibb_start(1, i)
    for i in range(NC):
        sibb_wait(1, i)


def write_out(x, s, r, p, x_hbm, s_hbm, r_hbm, p_hbm, sem):
    cps = []

    def store(src, dst):
        cp = pltpu.make_async_copy(src, dst, sem.at[len(cps)])
        cp.start()
        cps.append(cp)

    for t in range(NT):
        for h in range(2):
            rows = pl.ds(h * (S // 2), S // 2)
            store(x.at[t, rows], x_hbm.at[t, rows])
    for h in range(2):
        rows = pl.ds(h * (S // 2), S // 2)
        store(r.at[rows], r_hbm.at[rows])
    store(s, s_hbm)
    store(p, p_hbm)
    for cp in cps:
        cp.wait()


def shards(
    primal_start, supply_start, reach_start, spend_start, value, share, price, reach_cap,
    spend_limit, supply, eligible, start_slot, active_span,
):
    f32 = jnp.float32
    vmem = pl.BlockSpec(memory_space=pltpu.VMEM)
    anywhere = pl.BlockSpec(memory_space=pltpu.HBM)
    dma = pltpu.SemaphoreType.DMA
    outs = (
        pltpu.VMEM((NT, S, CD), f32),
        pltpu.VMEM((NT, S), f32),
        pltpu.VMEM((S, CD), f32),
        pltpu.VMEM((NT, CD), f32),
    )
    scratch = [
        pltpu.VMEM((NT, S), f32),
        pltpu.VMEM((NT, CD), f32),
        pltpu.VMEM((NL, 128), f32),
        pltpu.VMEM((NT, S), f32),
        pltpu.VMEM((S // SEG_BLOCK, CD), jnp.int32),
        pltpu.VMEM((NL, 128), jnp.int32),
        pltpu.VMEM((NL, 128), jnp.int32),
        pltpu.VMEM((NT, S, CD), f32),
        pltpu.VMEM((S, CD), f32),
        pltpu.VMEM((S, CD), f32),
        pltpu.VMEM((S, CD), f32),
        pltpu.VMEM((S, CD), f32),
        pltpu.VMEM((QR, CD), f32),
        pltpu.VMEM((2, NC, LT, S, 128), f32),
        pltpu.VMEM((2, NC, S, 128), f32),
        pltpu.VMEM((2, NC, 3, QR, 128), f32),
        pltpu.VMEM((NC, LT, S, 128), f32),
        pltpu.VMEM((S // SEG_BLOCK, 1, CD), f32),
        pltpu.VMEM((NT, S, 128), f32),
        pltpu.VMEM((8, S), f32),
        pltpu.VMEM((NT, S), f32),
        pltpu.VMEM((NT, S, 128), f32),
        pltpu.VMEM((2, 4, 8, S), f32),
        pltpu.VMEM((2, 4, 8, S), f32),
        pltpu.VMEM((NT, NL, 128), f32),
        pltpu.VMEM((NT, NL, 128), f32),
        pltpu.VMEM((NT, NL, 128), f32),
        pltpu.VMEM((NT, NL, 128), f32),
        pltpu.VMEM((NT, NL, 128), f32),
        pltpu.VMEM((2, NT, NL, 128), f32),
        pltpu.VMEM((8, NL, 128), f32),
        pltpu.VMEM((3, NG, 8, GL, 128), f32),
        dma((NT + 12,)),
        dma((2, NC)), dma((2, NC)),
        dma((2, NC, 3)), dma((2, NC, 3)),
        dma((2, NC, 3)), dma((2, NC, 3)),
        dma((2, NC)), dma((2, NC)),
        dma((7,)), dma((7,)),
        dma((3, NG, 7)), dma((3, NG, 7)),
        dma((2, 3)), dma((2, 3)),
        dma((2, 3)), dma((2, 3)),
    ]
    args = (
        primal_start, supply_start, reach_start, spend_start, value, share, price, reach_cap,
        spend_limit.reshape(NL, 128), supply, eligible,
        start_slot.reshape(NL, 128), active_span.reshape(NL, 128),
    )
    res = pl.pallas_call(
        kernel,
        out_shape=outs,
        in_specs=[anywhere] * 13,
        out_specs=(vmem,) * 4,
        scratch_shapes=scratch,
        compiler_params=pltpu.CompilerParams(
            collective_id=0, has_side_effects=True, vmem_limit_bytes=44 * 2**20
        ),
    )(*[pltpu.with_memory_space_constraint(a, pltpu.HBM) for a in args])
    return tuple(
        pl.pallas_call(
            write_out,
            out_shape=tuple(pltpu.HBM(o.shape, o.dtype) for o in outs),
            in_specs=[vmem] * 4,
            out_specs=(anywhere,) * 4,
            scratch_shapes=[dma((16,))],
            compiler_params=pltpu.CompilerParams(vmem_limit_bytes=2**20),
        )(*res)
    )


def solution(mesh):
    in_specs = (
        P("tm", None, "camp"), P("tm", None), P(None, "camp"), P("tm", "camp"),
        P(None, "camp"), P(None, "camp"), P(None, "camp"), P(None, "camp"),
        P("camp"), P("tm", None), P(None, "camp"), P("camp"), P("camp"),
    )
    out_specs = (P("tm", None, "camp"), P("tm", None), P(None, "camp"), P("tm", "camp"))
    return jax.shard_map(shards, mesh=mesh, in_specs=in_specs, out_specs=out_specs, check_vma=False)
```

```python
import jax
import jax.numpy as jnp
from jax import lax
from jax.experimental import pallas as pl
from jax.experimental.pallas import tpu as pltpu
from jax.sharding import PartitionSpec as P

S = 192
SEG_BLOCK = 8
SLOTS = 32
CAMPAIGNS = 32768
MESH = pl.DeviceIdType.MESH
HIGHEST = lax.Precision.HIGHEST

NT = 4
CD = 2048
NL = CD // 128
HL = 1
LT = 2 * HL
HW = HL * 128
NC = NL // LT
QR = S // 4
HR = QR // 2
NG = 2
GL = NL // NG
GC = NC // NG
BLOCKED = -1e30

SIG_SUPPLY = 4.0 / CAMPAIGNS
SIG_REACH = 1.0 / (2 * SLOTS)
SIG_SPEND = 1.0 / (S * SLOTS * SLOTS)


RS_RING = ((1,) * NC, (1,) * NC)
AG_RING = ((1,) * NC, (1,) * NC)


def make_order():
    o = []
    for i in range(NC):
        o.append(("comp", 0, i))
        if i >= 3:
            o.append(("rs1", 0, i - 3))
        if i == GC - 1:
            o.append(("sp1", 0, 0))
    o += [("uz", 0), ("sp1", 0, 1), ("rs1", 0, 5), ("rs1", 0, 6), ("rs1", 0, 7), ("caps",)]
    o += [("rs2", 0, 0), ("rs2", 0, 1), ("rs2", 0, 2), ("sp2", 0, 0)]
    o += [("rs2", 0, i) for i in range(3, 8)]
    o += [("uy", 0), ("ag1", 0, 0), ("ag1", 0, 1), ("sp2", 0, 1)]
    o += [("ag1", 0, i) for i in range(2, 8)]
    o += [("sp3", 0), ("ag2", 0, 0), ("ag2", 0, 1), ("ue", 0)]
    o += [("ag2", 0, i) for i in range(2, 6)]
    o += [("sibb", 0, 0), ("sibb", 0, 1), ("ag2", 0, 6), ("ag2", 0, 7), ("sp3", 1)]
    for i in range(NC):
        o.append(("fin", 0, i))
        o.append(("comp", 1, i))
        if i + 2 < NC:
            o.append(("sibb", 0, i + 2))
        if i >= 2:
            o.append(("rs1", 1, i - 2))
        if i == GC - 1:
            o.append(("sp1", 1, 0))
        if i >= 5:
            o.append(("rs2", 1, i - 5))
    o += [("rs1", 1, 6), ("rs1", 1, 7), ("uz", 1), ("sp1", 1, 1)]
    o += [("rs2", 1, i) for i in range(3, 8)]
    o += [("sp2", 1, 0)]
    o += [("ag1", 1, i) for i in range(0, 8)]
    o += [("uy", 1)]
    o += [("ag2", 1, i) for i in range(0, 8)]
    o += [("sp2", 1, 1), ("sibb", 1, 0), ("sibb", 1, 1), ("ue", 1)]
    o += [("sibb", 1, i) for i in range(2, 8)]
    o += [("fin", 1, i) for i in range(8)]
    return o


ORDER = make_order()


def kernel(
    x0_hbm, s0_hbm, r0_hbm, p0_hbm, value_hbm, share_hbm, price_hbm, rcap_hbm,
    limit_hbm, supply_hbm, elig_hbm, begin_hbm, span_hbm,
    x_ref, s_out, r_ref, p_out,
    s0_ref, p0_ref, limit_ref, supply_ref, elig_ref, begin_ref, span_ref,
    x0, value, share, price, r0, rcap,
    deliv, from_sib, ring, from_x, r1,
    pen, sb, s8, s1, used, uz, uy,
    pk0, pk1, cap, live, zeff, spent, tstart, tots,
    ld, sent, siba_r, rs1_r, rs2_r, ag1_r, ag2_r, sibb_r, t0_s, t0_r, tot_s, tot_r, used_s, used_r,
):
    camp = lax.axis_index("camp")
    tm = lax.axis_index("tm")
    y, z = camp // 4, camp % 4
    x, core = tm // 2, tm % 2
    sib = (camp, x * 2 + 1 - core)
    xs = [(camp, ((x + d) % 4) * 2 + core) for d in (1, 2, 3)]
    tms = [(camp, (tm + d) % 8) for d in range(1, 8)]
    zs = [(y * 4 + (z + d) % 4, tm) for d in (1, 2, 3)]
    ys = [(((y + d) % 4) * 4 + z, tm) for d in (1, 2, 3)]
    right, left = xs[0], xs[2]
    mine = pl.multiple_of(x * QR, 8)

    def wait_for(like, sem):
        pltpu.make_async_copy(like, like, sem).wait()

    def send(src, dst, ssem, rsem, to):
        return pltpu.make_async_remote_copy(
            src_ref=src, dst_ref=dst, send_sem=ssem, recv_sem=rsem, device_id=to, device_id_type=MESH
        )

    barrier = pltpu.get_barrier_semaphore()
    greet = tms + zs + ys
    for to in greet:
        pl.semaphore_signal(barrier, inc=1, device_id=to, device_id_type=MESH)

    loads = []

    def load(src, dst):
        cp = pltpu.make_async_copy(src, dst, ld.at[len(loads)])
        cp.start()
        loads.append(cp)

    for src, dst in (
        (p0_hbm, p0_ref), (s0_hbm, s0_ref), (elig_hbm, elig_ref), (begin_hbm, begin_ref),
        (span_hbm, span_ref), (limit_hbm, limit_ref), (supply_hbm, supply_ref),
    ):
        load(src, dst)
    small = len(loads)
    load(value_hbm, value)
    for t in range(NT):
        load(x0_hbm.at[t], x0.at[t])
    load(share_hbm, share)
    load(price_hbm, price)
    load(r0_hbm, r0)
    load(rcap_hbm.at[pl.ds(mine, QR)], rcap)

    for cp in loads[:small]:
        cp.wait()
    for t in range(NT):
        for lt in range(NL):
            pk0[t, lt : lt + 1, :] = p0_ref[t : t + 1, lt * 128 : (lt + 1) * 128]
    tstart[tm] = pk0[0] + pk0[1] + pk0[2] + pk0[3]

    def spread_supply(rows):
        s8[0:NT, :] = rows * -0.5
        table = s8[...]
        for t in range(NT):
            pick = (lax.broadcasted_iota(jnp.int32, (8, 128), 0) == t).astype(jnp.float32)
            sb[t] = lax.dot_general(
                table, pick, (((0,), (0,)), ((), ())), precision=HIGHEST, preferred_element_type=jnp.float32
            )

    begin = begin_ref[...]
    span = span_ref[...]
    for t in range(NT):
        slot = tm * NT + t
        live[t] = ((slot >= begin) & (slot < begin + span)).astype(jnp.float32)

    pl.semaphore_wait(barrier, len(greet))

    cps = [
        send(tstart.at[tm], tstart.at[tm], t0_s.at[0], t0_r.at[0], tms[d]) for d in range(7)
    ]
    for cp in cps:
        cp.start()

    s8[...] = jnp.zeros_like(s8)
    spread_supply(s0_ref[...])
    for b in range(S // SEG_BLOCK):
        pen[b] = jnp.where(elig_ref[b : b + 1, :] > 0, 0.0, BLOCKED)
    loads[small].wait()

    def value_body(rb, carry):
        rows = pl.ds(pl.multiple_of(rb * 8, 8), 8)
        value[rows, :] = 0.5 * value[rows, :] + pen[rb]
        return carry

    lax.fori_loop(0, S // 8, value_body, 0)
    used[...] = jnp.zeros_like(used)
    for cp in loads[small + 1 :]:
        cp.wait()

    def masked_total(parts, later):
        total = None
        for m in range(8):
            keep = (m > tm) if later else (m < tm)
            term = jnp.where(keep, parts(m), 0.0)
            total = term if total is None else total + term
        return total

    def set_zeff(duals, later, rows):
        run = later
        for t in reversed(range(NT)):
            run = run + duals[t]
            zeff[t, rows, :] = jnp.where(live[t, rows, :] > 0.0, -0.5 * run, BLOCKED)

    wait_for(tstart.at[pl.ds(0, 7)], t0_s.at[0])
    wait_for(tstart.at[pl.ds(0, 7)], t0_r.at[0])
    set_zeff(
        [pk0[t] for t in range(NT)],
        masked_total(lambda m: tstart[m], True),
        slice(0, NL),
    )

    def comp(it, i):
        zb = [
            [jnp.broadcast_to(zeff[t, i * LT + l : i * LT + l + 1, :], (8, 128)) for l in range(LT)]
            for t in range(NT)
        ]

        def body(rb, acc):
            rows = pl.ds(pl.multiple_of(rb * 8, 8), 8)
            acc = list(acc)
            uses = [None] * NT
            for l in range(LT):
                cols = pl.ds((i * LT + l) * 128, 128)
                sh = share[rows, cols]
                pr = price[rows, cols]
                rd = r0[rows, cols] if it == 0 else r1[rows, cols]
                base = value[rows, cols] - 0.5 * rd
                total = None
                for t in range(NT):
                    old = x0[t, rows, cols] if it == 0 else x_ref[t, rows, cols]
                    new = jnp.maximum((old + base) + (sh * sb[t, rows, :] + pr * zb[t][l]), 0.0)
                    bar = (new + new) - old
                    acc[t * LT + l] = acc[t * LT + l] + pr * bar
                    use = sh * bar
                    uses[t] = use if uses[t] is None else uses[t] + use
                    total = bar if total is None else total + bar
                    if it == 0:
                        x_ref[t, rows, cols] = new
                    else:
                        x_ref[t, rows, cols] = (2.0 / 3.0) * bar + (1.0 / 3.0) * x0[t, rows, cols]
                deliv[it, rows, cols] = total
            for t in range(NT):
                used[t, rows, :] = used[t, rows, :] + uses[t]
            return tuple(acc)

        zero = jnp.zeros((8, 128), jnp.float32)
        acc = lax.fori_loop(0, S // 8, body, (zero,) * (NT * LT), unroll=2)
        for t in range(NT):
            for l in range(LT):
                spent[it, t, i * LT + l : i * LT + l + 1, :] = jnp.sum(acc[t * LT + l], axis=0, keepdims=True)

    def half(i, core_of):
        return pl.ds(pl.multiple_of((i * LT + core_of * HL) * 128, 128), HW)

    def part(chip, first, rows):
        return pl.ds(pl.multiple_of(chip * QR + first, 8), rows)

    opposite, after, before = (x + 2) % 4, (x + 1) % 4, (x + 3) % 4
    whole_half = from_sib.at[0, :, pl.ds(0, HW)]

    def two(buf, rows, n=2):
        return buf.at[0, pl.ds(0, n), pl.ds(0, rows), pl.ds(0, HW)]

    def go(it, i, src, dst, rsem, to):
        send(src, dst, sent.at[it, i], rsem.at[i], to).start()

    def siba(it, i):
        cols = half(i, 1 - core)
        go(it, i, deliv.at[it, :, cols], from_sib.at[it, :, cols], siba_r, sib)

    def rs1(it, i):
        cols = half(i, core)
        wait_for(whole_half, siba_r.at[i])
        deliv[it, :, cols] = deliv[it, :, cols] + from_sib[it, :, cols]
        if RS_RING[it][i]:
            go(it, i, deliv.at[it, part(opposite, 0, HR), cols], ring.at[it, 0, :, cols], rs1_r, right)
            go(it, i, deliv.at[it, part(opposite, HR, HR), cols], ring.at[it, 1, :, cols], rs1_r, left)
        else:
            for d, chip, to in ((0, after, xs[0]), (1, before, xs[2]), (2, opposite, xs[1])):
                go(it, i, deliv.at[it, part(chip, 0, QR), cols], from_x.at[it, d, :, cols], rs2_r, to)

    def rs2(it, i):
        if RS_RING[it][i]:
            cols = half(i, core)
            wait_for(two(ring, HR), rs1_r.at[i])
            rows = part(after, 0, HR)
            deliv[it, rows, cols] = deliv[it, rows, cols] + ring[it, 0, :, cols]
            rows = part(before, HR, HR)
            deliv[it, rows, cols] = deliv[it, rows, cols] + ring[it, 1, :, cols]
            go(it, i, deliv.at[it, part(after, 0, QR), cols], from_x.at[it, 0, :, cols], rs2_r, right)
            go(it, i, deliv.at[it, part(before, 0, QR), cols], from_x.at[it, 1, :, cols], rs2_r, left)

    def ag1(it, i):
        cols = half(i, core)
        rows = part(x, 0, QR)
        wait_for(two(from_x, QR, 2 if RS_RING[it][i] else 3), rs2_r.at[i])
        total = deliv[it, rows, cols] + from_x[it, 0, :, cols] + from_x[it, 1, :, cols]
        if not RS_RING[it][i]:
            total = total + from_x[it, 2, :, cols]
        start = r0[rows, cols]
        if it == 0:
            r1[rows, cols] = jnp.maximum(start + SIG_REACH * (total - rcap[:, cols]), 0.0)
        else:
            old = r1[rows, cols]
            new = jnp.maximum(old + SIG_REACH * (total - rcap[:, cols]), 0.0)
            r_ref[rows, cols] = (2.0 / 3.0) * (2.0 * new - old) + (1.0 / 3.0) * start
        piece = (r1 if it == 0 else r_ref).at[rows, cols]
        go(it, i, piece, piece, ag1_r, right)
        go(it, i, piece, piece, ag1_r, left)
        if not AG_RING[it][i]:
            go(it, i, piece, piece, ag1_r, xs[1])

    def ag2(it, i):
        wait_for(two(from_x, QR, 2 if AG_RING[it][i] else 3), ag1_r.at[i])
        if AG_RING[it][i]:
            cols = half(i, core)
            out = r1 if it == 0 else r_ref
            piece = out.at[part(before, 0, HR), cols]
            go(it, i, piece, piece, ag2_r, right)
            piece = out.at[part(after, HR, HR), cols]
            go(it, i, piece, piece, ag2_r, left)

    def sibb(it, i):
        if AG_RING[it][i]:
            wait_for(two(ring, HR), ag2_r.at[i])
        out = r1 if it == 0 else r_ref
        piece = out.at[:, half(i, core)]
        go(it, i, piece, piece, sibb_r, sib)

    def fin(it, i):
        wait_for(whole_half, sibb_r.at[i])

    def all_sent():
        for it in range(2):
            for i in range(NC):
                wait_for(x0.at[0, pl.ds(0, 168), pl.ds(0, 4 * HW)], sent.at[it, i])

    def used_z(it):
        total = None
        for t in range(NT):
            term = lax.dot_general(
                jnp.ones((8, 128), jnp.float32), used[t], (((1,), (1,)), ((), ())),
                precision=HIGHEST, preferred_element_type=jnp.float32,
            )
            row = lax.broadcasted_iota(jnp.int32, (8, S), 0) == t
            term = jnp.where(row, term, 0.0)
            total = term if total is None else total + term
        uz[it, z] = total
        for to in zs:
            send(uz.at[it, z], uz.at[it, z], used_s.at[it, 0], used_r.at[it, 0], to).start()

    def used_y(it):
        for sem in (used_s, used_r):
            wait_for(uz.at[it, pl.ds(0, 3)], sem.at[it, 0])
        uy[it, y] = uz[it, 0] + uz[it, 1] + uz[it, 2] + uz[it, 3]
        for to in ys:
            send(uy.at[it, y], uy.at[it, y], used_s.at[it, 1], used_r.at[it, 1], to).start()

    def used_end(it):
        for sem in (used_s, used_r):
            wait_for(uy.at[it, pl.ds(0, 3)], sem.at[it, 1])
        total = uy[it, 0] + uy[it, 1] + uy[it, 2] + uy[it, 3]
        total = total[0:NT, :]
        if it == 0:
            new = jnp.maximum(s0_ref[...] + SIG_SUPPLY * (total - supply_ref[...]), 0.0)
            s1[...] = new
            spread_supply(new)
        else:
            old = s1[...]
            new = jnp.maximum(old + SIG_SUPPLY * (total - supply_ref[...]), 0.0)
            s_out[...] = (2.0 / 3.0) * (2.0 * new - old) + (1.0 / 3.0) * s0_ref[...]

    def share_total(e, g, value):
        tots[e, g, tm] = value
        for to in tms:
            send(tots.at[e, g, tm], tots.at[e, g, tm], tot_s.at[e, g], tot_r.at[e, g], to).start()

    def wait_total(e, g, later):
        for sem in (tot_s, tot_r):
            wait_for(tots.at[e, g, pl.ds(0, 7)], sem.at[e, g])
        return masked_total(lambda m: tots[e, g, m], later)

    def spend_1(it, g):
        rows = slice(g * GL, (g + 1) * GL)
        share_total(2 * it, g, spent[it, 0, rows] + spent[it, 1, rows] + spent[it, 2, rows] + spent[it, 3, rows])

    def spend_2(it, g):
        rows = slice(g * GL, (g + 1) * GL)
        run = wait_total(2 * it, g, False)
        fresh = []
        for t in range(NT):
            run = run + spent[it, t, rows]
            old = pk0[t, rows] if it == 0 else pk1[t, rows]
            new = jnp.maximum(old + SIG_SPEND * (run - cap[t, rows]), 0.0)
            if it == 0:
                pk1[t, rows] = new
                fresh.append(new)
            else:
                res = (2.0 / 3.0) * (2.0 * new - old) + (1.0 / 3.0) * pk0[t, rows]
                for lt in range(GL):
                    c = (g * GL + lt) * 128
                    p_out[t : t + 1, c : c + 128] = res[lt : lt + 1, :]
        if it == 0:
            share_total(1, g, fresh[0] + fresh[1] + fresh[2] + fresh[3])

    def spend_3(g):
        rows = slice(g * GL, (g + 1) * GL)
        later = wait_total(1, g, True)
        set_zeff([pk1[t, rows] for t in range(NT)], later, rows)

    def caps():
        for t in range(NT):
            frac = jnp.clip((tm * NT + t + 1 - begin).astype(jnp.float32) / span.astype(jnp.float32), 0.0, 1.0)
            cap[t] = limit_ref[...] * frac

    def new_supply(it):
        used_end(it)
        if it == 0:
            used[...] = jnp.zeros_like(used)

    def chunk(it, i):
        comp(it, i)
        siba(it, i)

    steps = dict(
        comp=chunk, rs1=rs1, rs2=rs2, ag1=ag1, ag2=ag2, sibb=sibb, fin=fin, uz=used_z, uy=used_y,
        ue=new_supply, sp1=spend_1, sp2=spend_2, sp3=spend_3, caps=caps,
    )
    for name, *where in ORDER:
        steps[name](*where)
    all_sent()


def write_out(x, s, r, p, x_hbm, s_hbm, r_hbm, p_hbm, sem):
    cps = []

    def store(src, dst):
        cp = pltpu.make_async_copy(src, dst, sem.at[len(cps)])
        cp.start()
        cps.append(cp)

    for t in range(NT):
        for h in range(2):
            rows = pl.ds(h * (S // 2), S // 2)
            store(x.at[t, rows], x_hbm.at[t, rows])
    for h in range(2):
        rows = pl.ds(h * (S // 2), S // 2)
        store(r.at[rows], r_hbm.at[rows])
    store(s, s_hbm)
    store(p, p_hbm)
    for cp in cps:
        cp.wait()


def shards(
    primal_start, supply_start, reach_start, spend_start, value, share, price, reach_cap,
    spend_limit, supply, eligible, start_slot, active_span,
):
    f32 = jnp.float32
    vmem = pl.BlockSpec(memory_space=pltpu.VMEM)
    anywhere = pl.BlockSpec(memory_space=pltpu.HBM)
    dma = pltpu.SemaphoreType.DMA
    outs = (
        pltpu.VMEM((NT, S, CD), f32),
        pltpu.VMEM((NT, S), f32),
        pltpu.VMEM((S, CD), f32),
        pltpu.VMEM((NT, CD), f32),
    )
    scratch = [
        pltpu.VMEM((NT, S), f32),
        pltpu.VMEM((NT, CD), f32),
        pltpu.VMEM((NL, 128), f32),
        pltpu.VMEM((NT, S), f32),
        pltpu.VMEM((S // SEG_BLOCK, CD), jnp.int32),
        pltpu.VMEM((NL, 128), jnp.int32),
        pltpu.VMEM((NL, 128), jnp.int32),
        pltpu.VMEM((NT, S, CD), f32),
        pltpu.VMEM((S, CD), f32),
        pltpu.VMEM((S, CD), f32),
        pltpu.VMEM((S, CD), f32),
        pltpu.VMEM((S, CD), f32),
        pltpu.VMEM((QR, CD), f32),
        pltpu.VMEM((2, S, CD), f32),
        pltpu.VMEM((2, S, CD), f32),
        pltpu.VMEM((2, 2, HR, CD), f32),
        pltpu.VMEM((2, 3, QR, CD), f32),
        pltpu.VMEM((S, CD), f32),
        pltpu.VMEM((S // SEG_BLOCK, 1, CD), f32),
        pltpu.VMEM((NT, S, 128), f32),
        pltpu.VMEM((8, S), f32),
        pltpu.VMEM((NT, S), f32),
        pltpu.VMEM((NT, S, 128), f32),
        pltpu.VMEM((2, 4, 8, S), f32),
        pltpu.VMEM((2, 4, 8, S), f32),
        pltpu.VMEM((NT, NL, 128), f32),
        pltpu.VMEM((NT, NL, 128), f32),
        pltpu.VMEM((NT, NL, 128), f32),
        pltpu.VMEM((NT, NL, 128), f32),
        pltpu.VMEM((NT, NL, 128), f32),
        pltpu.VMEM((2, NT, NL, 128), f32),
        pltpu.VMEM((8, NL, 128), f32),
        pltpu.VMEM((3, NG, 8, GL, 128), f32),
        dma((NT + 12,)),
        dma((2, NC)),
        dma((NC,)), dma((NC,)), dma((NC,)), dma((NC,)), dma((NC,)), dma((NC,)),
        dma((1,)), dma((1,)),
        dma((3, NG)), dma((3, NG)),
        dma((2, 2)), dma((2, 2)),
    ]
    args = (
        primal_start, supply_start, reach_start, spend_start, value, share, price, reach_cap,
        spend_limit.reshape(NL, 128), supply, eligible,
        start_slot.reshape(NL, 128), active_span.reshape(NL, 128),
    )
    res = pl.pallas_call(
        kernel,
        out_shape=outs,
        in_specs=[anywhere] * 13,
        out_specs=(vmem,) * 4,
        scratch_shapes=scratch,
        compiler_params=pltpu.CompilerParams(
            collective_id=0, has_side_effects=True, vmem_limit_bytes=44 * 2**20
        ),
    )(*[pltpu.with_memory_space_constraint(a, pltpu.HBM) for a in args])
    return tuple(
        pl.pallas_call(
            write_out,
            out_shape=tuple(pltpu.HBM(o.shape, o.dtype) for o in outs),
            in_specs=[vmem] * 4,
            out_specs=(anywhere,) * 4,
            scratch_shapes=[dma((16,))],
            compiler_params=pltpu.CompilerParams(vmem_limit_bytes=2**20),
        )(*res)
    )


def solution(mesh):
    in_specs = (
        P("tm", None, "camp"), P("tm", None), P(None, "camp"), P("tm", "camp"),
        P(None, "camp"), P(None, "camp"), P(None, "camp"), P(None, "camp"),
        P("camp"), P("tm", None), P(None, "camp"), P("camp"), P("camp"),
    )
    out_specs = (P("tm", None, "camp"), P("tm", None), P(None, "camp"), P("tm", "camp"))
    return jax.shard_map(shards, mesh=mesh, in_specs=in_specs, out_specs=out_specs, check_vma=False)
```

```python
import jax
import jax.numpy as jnp
from jax import lax
from jax.experimental import pallas as pl
from jax.experimental.pallas import tpu as pltpu
from jax.sharding import PartitionSpec as P

S = 192
SEG_BLOCK = 8
SLOTS = 32
CAMPAIGNS = 32768
MESH = pl.DeviceIdType.MESH
HIGHEST = lax.Precision.HIGHEST

NT = 4
CD = 2048
NL = CD // 128
HL = 1
LT = 2 * HL
HW = HL * 128
NC = NL // LT
QR = S // 4
HR = QR // 2
NG = 2
GL = NL // NG
GC = NC // NG
BLOCKED = -1e30

SIG_SUPPLY = 4.0 / CAMPAIGNS
SIG_REACH = 1.0 / (2 * SLOTS)
SIG_SPEND = 1.0 / (S * SLOTS * SLOTS)


RS_RING = ((1, 1, 1, 1, 1, 1, 0, 0), (0, 0, 0, 0, 0, 0, 0, 1))
AG_RING = ((1, 0, 0, 0, 0, 0, 0, 1), (0, 1, 1, 1, 0, 1, 1, 1))
ORDER = (
    ("comp", 0, 5), ("comp", 0, 6), ("comp", 0, 7), ("comp", 0, 4), ("rs1", 0, 5), ("sp1", 0, 1),
    ("comp", 0, 1), ("rs1", 0, 6), ("rs1", 0, 7), ("caps",), ("comp", 0, 0), ("comp", 0, 3), ("comp", 0, 2),
    ("rs1", 0, 1), ("uz", 0), ("rs1", 0, 4), ("rs1", 0, 2), ("rs1", 0, 3), ("rs1", 0, 0), ("rs2", 0, 5),
    ("sp2", 0, 1), ("sp1", 0, 0), ("ag1", 0, 6), ("ag1", 0, 7), ("rs2", 0, 1), ("rs2", 0, 3), ("ag1", 0, 5),
    ("uy", 0), ("rs2", 0, 0), ("rs2", 0, 2), ("rs2", 0, 4), ("ag2", 0, 7), ("sibb", 0, 6), ("ag1", 0, 1),
    ("fin", 0, 6), ("ag1", 0, 3), ("sibb", 0, 5), ("sp2", 0, 0), ("sp3", 1), ("ue", 0), ("ag1", 0, 0),
    ("comp", 1, 6), ("ag1", 0, 2), ("fin", 0, 5), ("sibb", 0, 7), ("comp", 1, 5), ("ag1", 0, 4),
    ("rs1", 1, 5), ("rs1", 1, 6), ("sibb", 0, 1), ("fin", 0, 7), ("comp", 1, 7), ("sibb", 0, 3), ("sp3", 0),
    ("fin", 0, 1), ("comp", 1, 1), ("ag2", 0, 0), ("fin", 0, 3), ("comp", 1, 3), ("rs1", 1, 7),
    ("sibb", 0, 2), ("rs1", 1, 1), ("rs1", 1, 3), ("sibb", 0, 4), ("fin", 0, 2), ("comp", 1, 2),
    ("ag1", 1, 5), ("fin", 0, 4), ("comp", 1, 4), ("rs1", 1, 2), ("sibb", 0, 0), ("rs2", 1, 7), ("rs1", 1, 4),
    ("fin", 0, 0), ("comp", 1, 0), ("ag1", 1, 1), ("uz", 1), ("rs1", 1, 0), ("ag1", 1, 3), ("ag1", 1, 2),
    ("ag1", 1, 7), ("ag1", 1, 6), ("ag2", 1, 5), ("uy", 1), ("ag2", 1, 1), ("ag1", 1, 4), ("ag1", 1, 0),
    ("ag2", 1, 2), ("ag2", 1, 3), ("ag2", 1, 7), ("ue", 1), ("ag2", 1, 6), ("sp1", 1, 1), ("sibb", 1, 5),
    ("sp1", 1, 0), ("sibb", 1, 1), ("fin", 1, 5), ("fin", 1, 1), ("sibb", 1, 4), ("sibb", 1, 0),
    ("sibb", 1, 2), ("sibb", 1, 3), ("fin", 1, 4), ("sibb", 1, 7), ("sibb", 1, 6), ("fin", 1, 0),
    ("fin", 1, 2), ("fin", 1, 7), ("fin", 1, 3), ("sp2", 1, 1), ("sp2", 1, 0), ("fin", 1, 6),
)


def kernel(
    x0_hbm, s0_hbm, r0_hbm, p0_hbm, value_hbm, share_hbm, price_hbm, rcap_hbm,
    limit_hbm, supply_hbm, elig_hbm, begin_hbm, span_hbm,
    x_ref, s_out, r_ref, p_out,
    s0_ref, p0_ref, limit_ref, supply_ref, elig_ref, begin_ref, span_ref,
    x0, value, share, price, r0, rcap,
    deliv, from_sib, ring, from_x, r1,
    pen, sb, s8, s1, used, uz, uy,
    pk0, pk1, cap, live, zeff, spent, tstart, tots,
    ld, sent, siba_r, rs1_r, rs2_r, ag1_r, ag2_r, sibb_r, t0_s, t0_r, tot_s, tot_r, used_s, used_r,
):
    camp = lax.axis_index("camp")
    tm = lax.axis_index("tm")
    y, z = camp // 4, camp % 4
    x, core = tm // 2, tm % 2
    sib = (camp, x * 2 + 1 - core)
    xs = [(camp, ((x + d) % 4) * 2 + core) for d in (1, 2, 3)]
    tms = [(camp, (tm + d) % 8) for d in range(1, 8)]
    zs = [(y * 4 + (z + d) % 4, tm) for d in (1, 2, 3)]
    ys = [(((y + d) % 4) * 4 + z, tm) for d in (1, 2, 3)]
    right, left = xs[0], xs[2]
    mine = pl.multiple_of(x * QR, 8)

    def wait_for(like, sem):
        pltpu.make_async_copy(like, like, sem).wait()

    def send(src, dst, ssem, rsem, to):
        return pltpu.make_async_remote_copy(
            src_ref=src, dst_ref=dst, send_sem=ssem, recv_sem=rsem, device_id=to, device_id_type=MESH
        )

    barrier = pltpu.get_barrier_semaphore()
    greet = tms + zs + ys
    for to in greet:
        pl.semaphore_signal(barrier, inc=1, device_id=to, device_id_type=MESH)

    loads = []

    def load(src, dst):
        cp = pltpu.make_async_copy(src, dst, ld.at[len(loads)])
        cp.start()
        loads.append(cp)

    for src, dst in (
        (p0_hbm, p0_ref), (s0_hbm, s0_ref), (elig_hbm, elig_ref), (begin_hbm, begin_ref),
        (span_hbm, span_ref), (limit_hbm, limit_ref), (supply_hbm, supply_ref),
    ):
        load(src, dst)
    small = len(loads)
    load(value_hbm, value)
    for t in range(NT):
        load(x0_hbm.at[t], x0.at[t])
    load(share_hbm, share)
    load(price_hbm, price)
    load(r0_hbm, r0)
    load(rcap_hbm.at[pl.ds(mine, QR)], rcap)

    for cp in loads[:small]:
        cp.wait()
    for t in range(NT):
        for lt in range(NL):
            pk0[t, lt : lt + 1, :] = p0_ref[t : t + 1, lt * 128 : (lt + 1) * 128]
    tstart[tm] = pk0[0] + pk0[1] + pk0[2] + pk0[3]

    def spread_supply(rows):
        s8[0:NT, :] = rows * -0.5
        table = s8[...]
        for t in range(NT):
            pick = (lax.broadcasted_iota(jnp.int32, (8, 128), 0) == t).astype(jnp.float32)
            sb[t] = lax.dot_general(
                table, pick, (((0,), (0,)), ((), ())), precision=HIGHEST, preferred_element_type=jnp.float32
            )

    begin = begin_ref[...]
    span = span_ref[...]
    for t in range(NT):
        slot = tm * NT + t
        live[t] = ((slot >= begin) & (slot < begin + span)).astype(jnp.float32)

    pl.semaphore_wait(barrier, len(greet))

    cps = [
        send(tstart.at[tm], tstart.at[tm], t0_s.at[0], t0_r.at[0], tms[d]) for d in range(7)
    ]
    for cp in cps:
        cp.start()

    s8[...] = jnp.zeros_like(s8)
    spread_supply(s0_ref[...])
    for b in range(S // SEG_BLOCK):
        pen[b] = jnp.where(elig_ref[b : b + 1, :] > 0, 0.0, BLOCKED)
    loads[small].wait()

    def value_body(rb, carry):
        rows = pl.ds(pl.multiple_of(rb * 8, 8), 8)
        value[rows, :] = 0.5 * value[rows, :] + pen[rb]
        return carry

    lax.fori_loop(0, S // 8, value_body, 0)
    used[...] = jnp.zeros_like(used)
    for cp in loads[small + 1 :]:
        cp.wait()

    def masked_total(parts, later):
        total = None
        for m in range(8):
            keep = (m > tm) if later else (m < tm)
            term = jnp.where(keep, parts(m), 0.0)
            total = term if total is None else total + term
        return total

    def set_zeff(duals, later, rows):
        run = later
        for t in reversed(range(NT)):
            run = run + duals[t]
            zeff[t, rows, :] = jnp.where(live[t, rows, :] > 0.0, -0.5 * run, BLOCKED)

    wait_for(tstart.at[pl.ds(0, 7)], t0_s.at[0])
    wait_for(tstart.at[pl.ds(0, 7)], t0_r.at[0])
    set_zeff(
        [pk0[t] for t in range(NT)],
        masked_total(lambda m: tstart[m], True),
        slice(0, NL),
    )

    def comp(it, i):
        zb = [
            [jnp.broadcast_to(zeff[t, i * LT + l : i * LT + l + 1, :], (8, 128)) for l in range(LT)]
            for t in range(NT)
        ]

        def body(rb, acc):
            rows = pl.ds(pl.multiple_of(rb * 8, 8), 8)
            acc = list(acc)
            uses = [None] * NT
            for l in range(LT):
                cols = pl.ds((i * LT + l) * 128, 128)
                sh = share[rows, cols]
                pr = price[rows, cols]
                rd = r0[rows, cols] if it == 0 else r1[rows, cols]
                base = value[rows, cols] - 0.5 * rd
                total = None
                for t in range(NT):
                    old = x0[t, rows, cols] if it == 0 else x_ref[t, rows, cols]
                    new = jnp.maximum((old + base) + (sh * sb[t, rows, :] + pr * zb[t][l]), 0.0)
                    bar = (new + new) - old
                    acc[t * LT + l] = acc[t * LT + l] + pr * bar
                    use = sh * bar
                    uses[t] = use if uses[t] is None else uses[t] + use
                    total = bar if total is None else total + bar
                    if it == 0:
                        x_ref[t, rows, cols] = new
                    else:
                        x_ref[t, rows, cols] = (2.0 / 3.0) * bar + (1.0 / 3.0) * x0[t, rows, cols]
                deliv[it, rows, cols] = total
            for t in range(NT):
                used[t, rows, :] = used[t, rows, :] + uses[t]
            return tuple(acc)

        zero = jnp.zeros((8, 128), jnp.float32)
        acc = lax.fori_loop(0, S // 8, body, (zero,) * (NT * LT), unroll=2)
        for t in range(NT):
            for l in range(LT):
                spent[it, t, i * LT + l : i * LT + l + 1, :] = jnp.sum(acc[t * LT + l], axis=0, keepdims=True)

    def half(i, core_of):
        return pl.ds(pl.multiple_of((i * LT + core_of * HL) * 128, 128), HW)

    def part(chip, first, rows):
        return pl.ds(pl.multiple_of(chip * QR + first, 8), rows)

    opposite, after, before = (x + 2) % 4, (x + 1) % 4, (x + 3) % 4
    whole_half = from_sib.at[0, :, pl.ds(0, HW)]

    def two(buf, rows, n=2):
        return buf.at[0, pl.ds(0, n), pl.ds(0, rows), pl.ds(0, HW)]

    def go(it, i, src, dst, rsem, to):
        send(src, dst, sent.at[it, i], rsem.at[i], to).start()

    def siba(it, i):
        cols = half(i, 1 - core)
        go(it, i, deliv.at[it, :, cols], from_sib.at[it, :, cols], siba_r, sib)

    def rs1(it, i):
        cols = half(i, core)
        wait_for(whole_half, siba_r.at[i])
        deliv[it, :, cols] = deliv[it, :, cols] + from_sib[it, :, cols]
        if RS_RING[it][i]:
            go(it, i, deliv.at[it, part(opposite, 0, HR), cols], ring.at[it, 0, :, cols], rs1_r, right)
            go(it, i, deliv.at[it, part(opposite, HR, HR), cols], ring.at[it, 1, :, cols], rs1_r, left)
        else:
            for d, chip, to in ((0, after, xs[0]), (1, before, xs[2]), (2, opposite, xs[1])):
                go(it, i, deliv.at[it, part(chip, 0, QR), cols], from_x.at[it, d, :, cols], rs2_r, to)

    def rs2(it, i):
        cols = half(i, core)
        wait_for(two(ring, HR), rs1_r.at[i])
        rows = part(after, 0, HR)
        deliv[it, rows, cols] = deliv[it, rows, cols] + ring[it, 0, :, cols]
        rows = part(before, HR, HR)
        deliv[it, rows, cols] = deliv[it, rows, cols] + ring[it, 1, :, cols]
        go(it, i, deliv.at[it, part(after, 0, QR), cols], from_x.at[it, 0, :, cols], rs2_r, right)
        go(it, i, deliv.at[it, part(before, 0, QR), cols], from_x.at[it, 1, :, cols], rs2_r, left)

    def ag1(it, i):
        cols = half(i, core)
        rows = part(x, 0, QR)
        wait_for(two(from_x, QR, 2 if RS_RING[it][i] else 3), rs2_r.at[i])
        total = deliv[it, rows, cols] + from_x[it, 0, :, cols] + from_x[it, 1, :, cols]
        if not RS_RING[it][i]:
            total = total + from_x[it, 2, :, cols]
        start = r0[rows, cols]
        if it == 0:
            r1[rows, cols] = jnp.maximum(start + SIG_REACH * (total - rcap[:, cols]), 0.0)
        else:
            old = r1[rows, cols]
            new = jnp.maximum(old + SIG_REACH * (total - rcap[:, cols]), 0.0)
            r_ref[rows, cols] = (2.0 / 3.0) * (2.0 * new - old) + (1.0 / 3.0) * start
        piece = (r1 if it == 0 else r_ref).at[rows, cols]
        go(it, i, piece, piece, ag1_r, right)
        go(it, i, piece, piece, ag1_r, left)
        if not AG_RING[it][i]:
            go(it, i, piece, piece, ag1_r, xs[1])

    def ag2(it, i):
        wait_for(two(from_x, QR), ag1_r.at[i])
        cols = half(i, core)
        out = r1 if it == 0 else r_ref
        piece = out.at[part(before, 0, HR), cols]
        go(it, i, piece, piece, ag2_r, right)
        piece = out.at[part(after, HR, HR), cols]
        go(it, i, piece, piece, ag2_r, left)

    def sibb(it, i):
        if AG_RING[it][i]:
            wait_for(two(ring, HR), ag2_r.at[i])
        else:
            wait_for(two(from_x, QR, 3), ag1_r.at[i])
        out = r1 if it == 0 else r_ref
        piece = out.at[:, half(i, core)]
        go(it, i, piece, piece, sibb_r, sib)

    def fin(it, i):
        wait_for(whole_half, sibb_r.at[i])

    def all_sent():
        for it in range(2):
            for i in range(NC):
                wait_for(x0.at[0, pl.ds(0, 168), pl.ds(0, 4 * HW)], sent.at[it, i])

    def used_z(it):
        total = None
        for t in range(NT):
            term = lax.dot_general(
                jnp.ones((8, 128), jnp.float32), used[t], (((1,), (1,)), ((), ())),
                precision=HIGHEST, preferred_element_type=jnp.float32,
            )
            row = lax.broadcasted_iota(jnp.int32, (8, S), 0) == t
            term = jnp.where(row, term, 0.0)
            total = term if total is None else total + term
        uz[it, z] = total
        for to in zs:
            send(uz.at[it, z], uz.at[it, z], used_s.at[it, 0], used_r.at[it, 0], to).start()

    def used_y(it):
        for sem in (used_s, used_r):
            wait_for(uz.at[it, pl.ds(0, 3)], sem.at[it, 0])
        uy[it, y] = uz[it, 0] + uz[it, 1] + uz[it, 2] + uz[it, 3]
        for to in ys:
            send(uy.at[it, y], uy.at[it, y], used_s.at[it, 1], used_r.at[it, 1], to).start()

    def used_end(it):
        for sem in (used_s, used_r):
            wait_for(uy.at[it, pl.ds(0, 3)], sem.at[it, 1])
        total = uy[it, 0] + uy[it, 1] + uy[it, 2] + uy[it, 3]
        total = total[0:NT, :]
        if it == 0:
            new = jnp.maximum(s0_ref[...] + SIG_SUPPLY * (total - supply_ref[...]), 0.0)
            s1[...] = new
            spread_supply(new)
        else:
            old = s1[...]
            new = jnp.maximum(old + SIG_SUPPLY * (total - supply_ref[...]), 0.0)
            s_out[...] = (2.0 / 3.0) * (2.0 * new - old) + (1.0 / 3.0) * s0_ref[...]

    def share_total(e, g, value):
        tots[e, g, tm] = value
        for to in tms:
            send(tots.at[e, g, tm], tots.at[e, g, tm], tot_s.at[e, g], tot_r.at[e, g], to).start()

    def wait_total(e, g, later):
        for sem in (tot_s, tot_r):
            wait_for(tots.at[e, g, pl.ds(0, 7)], sem.at[e, g])
        return masked_total(lambda m: tots[e, g, m], later)

    def spend_1(it, g):
        rows = slice(g * GL, (g + 1) * GL)
        share_total(2 * it, g, spent[it, 0, rows] + spent[it, 1, rows] + spent[it, 2, rows] + spent[it, 3, rows])

    def spend_2(it, g):
        rows = slice(g * GL, (g + 1) * GL)
        run = wait_total(2 * it, g, False)
        fresh = []
        for t in range(NT):
            run = run + spent[it, t, rows]
            old = pk0[t, rows] if it == 0 else pk1[t, rows]
            new = jnp.maximum(old + SIG_SPEND * (run - cap[t, rows]), 0.0)
            if it == 0:
                pk1[t, rows] = new
                fresh.append(new)
            else:
                res = (2.0 / 3.0) * (2.0 * new - old) + (1.0 / 3.0) * pk0[t, rows]
                for lt in range(GL):
                    c = (g * GL + lt) * 128
                    p_out[t : t + 1, c : c + 128] = res[lt : lt + 1, :]
        if it == 0:
            share_total(1, g, fresh[0] + fresh[1] + fresh[2] + fresh[3])

    def spend_3(g):
        rows = slice(g * GL, (g + 1) * GL)
        later = wait_total(1, g, True)
        set_zeff([pk1[t, rows] for t in range(NT)], later, rows)

    def caps():
        for t in range(NT):
            frac = jnp.clip((tm * NT + t + 1 - begin).astype(jnp.float32) / span.astype(jnp.float32), 0.0, 1.0)
            cap[t] = limit_ref[...] * frac

    def new_supply(it):
        used_end(it)
        if it == 0:
            used[...] = jnp.zeros_like(used)

    def chunk(it, i):
        comp(it, i)
        siba(it, i)

    steps = dict(
        comp=chunk, rs1=rs1, rs2=rs2, ag1=ag1, ag2=ag2, sibb=sibb, fin=fin, uz=used_z, uy=used_y,
        ue=new_supply, sp1=spend_1, sp2=spend_2, sp3=spend_3, caps=caps,
    )
    for name, *where in ORDER:
        steps[name](*where)
    all_sent()


def write_out(x, s, r, p, x_hbm, s_hbm, r_hbm, p_hbm, sem):
    cps = []

    def store(src, dst):
        cp = pltpu.make_async_copy(src, dst, sem.at[len(cps)])
        cp.start()
        cps.append(cp)

    for t in range(NT):
        for h in range(2):
            rows = pl.ds(h * (S // 2), S // 2)
            store(x.at[t, rows], x_hbm.at[t, rows])
    for h in range(2):
        rows = pl.ds(h * (S // 2), S // 2)
        store(r.at[rows], r_hbm.at[rows])
    store(s, s_hbm)
    store(p, p_hbm)
    for cp in cps:
        cp.wait()


def shards(
    primal_start, supply_start, reach_start, spend_start, value, share, price, reach_cap,
    spend_limit, supply, eligible, start_slot, active_span,
):
    f32 = jnp.float32
    vmem = pl.BlockSpec(memory_space=pltpu.VMEM)
    anywhere = pl.BlockSpec(memory_space=pltpu.HBM)
    dma = pltpu.SemaphoreType.DMA
    outs = (
        pltpu.VMEM((NT, S, CD), f32),
        pltpu.VMEM((NT, S), f32),
        pltpu.VMEM((S, CD), f32),
        pltpu.VMEM((NT, CD), f32),
    )
    scratch = [
        pltpu.VMEM((NT, S), f32),
        pltpu.VMEM((NT, CD), f32),
        pltpu.VMEM((NL, 128), f32),
        pltpu.VMEM((NT, S), f32),
        pltpu.VMEM((S // SEG_BLOCK, CD), jnp.int32),
        pltpu.VMEM((NL, 128), jnp.int32),
        pltpu.VMEM((NL, 128), jnp.int32),
        pltpu.VMEM((NT, S, CD), f32),
        pltpu.VMEM((S, CD), f32),
        pltpu.VMEM((S, CD), f32),
        pltpu.VMEM((S, CD), f32),
        pltpu.VMEM((S, CD), f32),
        pltpu.VMEM((QR, CD), f32),
        pltpu.VMEM((2, S, CD), f32),
        pltpu.VMEM((2, S, CD), f32),
        pltpu.VMEM((2, 2, HR, CD), f32),
        pltpu.VMEM((2, 3, QR, CD), f32),
        pltpu.VMEM((S, CD), f32),
        pltpu.VMEM((S // SEG_BLOCK, 1, CD), f32),
        pltpu.VMEM((NT, S, 128), f32),
        pltpu.VMEM((8, S), f32),
        pltpu.VMEM((NT, S), f32),
        pltpu.VMEM((NT, S, 128), f32),
        pltpu.VMEM((2, 4, 8, S), f32),
        pltpu.VMEM((2, 4, 8, S), f32),
        pltpu.VMEM((NT, NL, 128), f32),
        pltpu.VMEM((NT, NL, 128), f32),
        pltpu.VMEM((NT, NL, 128), f32),
        pltpu.VMEM((NT, NL, 128), f32),
        pltpu.VMEM((NT, NL, 128), f32),
        pltpu.VMEM((2, NT, NL, 128), f32),
        pltpu.VMEM((8, NL, 128), f32),
        pltpu.VMEM((3, NG, 8, GL, 128), f32),
        dma((NT + 12,)),
        dma((2, NC)),
        dma((NC,)), dma((NC,)), dma((NC,)), dma((NC,)), dma((NC,)), dma((NC,)),
        dma((1,)), dma((1,)),
        dma((3, NG)), dma((3, NG)),
        dma((2, 2)), dma((2, 2)),
    ]
    args = (
        primal_start, supply_start, reach_start, spend_start, value, share, price, reach_cap,
        spend_limit.reshape(NL, 128), supply, eligible,
        start_slot.reshape(NL, 128), active_span.reshape(NL, 128),
    )
    res = pl.pallas_call(
        kernel,
        out_shape=outs,
        in_specs=[anywhere] * 13,
        out_specs=(vmem,) * 4,
        scratch_shapes=scratch,
        compiler_params=pltpu.CompilerParams(
            collective_id=0, has_side_effects=True, vmem_limit_bytes=44 * 2**20
        ),
    )(*[pltpu.with_memory_space_constraint(a, pltpu.HBM) for a in args])
    return tuple(
        pl.pallas_call(
            write_out,
            out_shape=tuple(pltpu.HBM(o.shape, o.dtype) for o in outs),
            in_specs=[vmem] * 4,
            out_specs=(anywhere,) * 4,
            scratch_shapes=[dma((16,))],
            compiler_params=pltpu.CompilerParams(vmem_limit_bytes=2**20),
        )(*res)
    )


def solution(mesh):
    in_specs = (
        P("tm", None, "camp"), P("tm", None), P(None, "camp"), P("tm", "camp"),
        P(None, "camp"), P(None, "camp"), P(None, "camp"), P(None, "camp"),
        P("camp"), P("tm", None), P(None, "camp"), P("camp"), P("camp"),
    )
    out_specs = (P("tm", None, "camp"), P("tm", None), P(None, "camp"), P("tm", "camp"))
    return jax.shard_map(shards, mesh=mesh, in_specs=in_specs, out_specs=out_specs, check_vma=False)
```

```python
import jax
import jax.numpy as jnp
from jax import lax
from jax.experimental import pallas as pl
from jax.experimental.pallas import tpu as pltpu
from jax.sharding import PartitionSpec as P

S = 192
SEG_BLOCK = 8
SLOTS = 32
CAMPAIGNS = 32768
MESH = pl.DeviceIdType.MESH
HIGHEST = lax.Precision.HIGHEST

NT = 4
NU = 2 * NT
CD = 2048
CW = CD // 2
NC = CW // 128
QR = S // 4
HR = QR // 2
NG = 2
GC = NC // NG
BLOCKED = -1e30

SIG_SUPPLY = 4.0 / CAMPAIGNS
SIG_REACH = 1.0 / (2 * SLOTS)
SIG_SPEND = 1.0 / (S * SLOTS * SLOTS)

RS_RING = ((0, 0, 0, 1, 1, 1, 1, 0), (1, 0, 1, 0, 1, 0, 0, 1))
AG_RING = ((1, 0, 0, 0, 0, 0, 0, 1), (0, 1, 1, 1, 0, 1, 1, 0))
ORDER = (
    ("comp", 0, 0), ("rs1", 0, 0), ("comp", 0, 6), ("comp", 0, 7), ("rs1", 0, 6), ("rs1", 0, 7), ("caps",),
    ("comp", 0, 5), ("comp", 0, 3), ("rs1", 0, 3), ("comp", 0, 4), ("sp1", 0, 1), ("rs1", 0, 4),
    ("rs1", 0, 5), ("comp", 0, 2), ("rs1", 0, 2), ("comp", 0, 1), ("uz", 0), ("rs1", 0, 1), ("rs2", 0, 6),
    ("ag1", 0, 0), ("sp1", 0, 0), ("ag1", 0, 7), ("rs2", 0, 5), ("uy", 0), ("rs2", 0, 4), ("ag1", 0, 2),
    ("rs2", 0, 3), ("sp2", 0, 1), ("ag1", 0, 6), ("ag2", 0, 0), ("sp2", 0, 0), ("ag2", 0, 7), ("ag1", 0, 1),
    ("us", 0), ("ag1", 0, 4), ("fin", 0, 2), ("ag1", 0, 5), ("ag1", 0, 3), ("ue", 0), ("fin", 0, 6),
    ("sp3", 1), ("comp", 1, 6), ("rs1", 1, 6), ("sp3", 0), ("fin", 0, 7), ("fin", 0, 0), ("comp", 1, 2),
    ("comp", 1, 7), ("rs1", 1, 7), ("fin", 0, 1), ("comp", 1, 1), ("rs1", 1, 2), ("rs1", 1, 1), ("fin", 0, 4),
    ("comp", 1, 4), ("rs1", 1, 4), ("comp", 1, 0), ("rs1", 1, 0), ("fin", 0, 5), ("comp", 1, 5),
    ("rs1", 1, 5), ("fin", 0, 3), ("comp", 1, 3), ("rs1", 1, 3), ("xo", 0, 8), ("ag1", 1, 6), ("rs2", 1, 2),
    ("rs2", 1, 4), ("rs2", 1, 7), ("ag1", 1, 1), ("rs2", 1, 0), ("ag1", 1, 5), ("uz", 1), ("ag1", 1, 3),
    ("ag2", 1, 6), ("ag1", 1, 2), ("ag1", 1, 4), ("ag2", 1, 1), ("ag1", 1, 7), ("uy", 1), ("ag1", 1, 0),
    ("ag2", 1, 5), ("ag2", 1, 3), ("sibb", 1, 6), ("ag2", 1, 2), ("sp1", 1, 0), ("sp1", 1, 1), ("fin", 1, 6),
    ("sibb", 1, 1), ("sibb", 1, 4), ("sibb", 1, 7), ("fin", 1, 1), ("us", 1), ("fin", 1, 4), ("sibb", 1, 0),
    ("sibb", 1, 5), ("sibb", 1, 3), ("sibb", 1, 2), ("fin", 1, 7), ("fin", 1, 0), ("sp2", 1, 0),
    ("fin", 1, 5), ("ue", 1), ("sp2", 1, 1), ("pf1",), ("fin", 1, 3), ("fin", 1, 2), ("pf2",),
)


FIRST = [where[1] for name, *where in ORDER if name == "comp" and where[0] == 0]


def kernel(
    x0_hbm, s0_hbm, r0_hbm, p0_hbm, value_hbm, share_hbm, price_hbm, rcap_hbm,
    limit_hbm, supply_hbm, elig_hbm, begin_hbm, span_hbm,
    x_out, s_out, r_out, p_out,
    p0_ref, limit_ref, elig_ref, begin_ref, span_ref, rows_ref,
    x0, x1, value, share, price, r0, rcap,
    deliv, ring, from_x, r1,
    pen, sb, s8, s1, used, uz, uy, us,
    pka, pk0, pk1, pres, pin, cap, live, zeff, spent, tsum, tstart, tots,
    ld, x_s, x_r, xo, start_s, start_r, sent, rs1_r, rs2_r, ag1_r, ag2_r, sibb_r,
    tot_s, tot_r, used_s, used_r, pf,
):
    camp = lax.axis_index("camp")
    tm = lax.axis_index("tm")
    y, z = camp // 4, camp % 4
    x, core = tm // 2, tm % 2
    other = 1 - core
    sib = (camp, x * 2 + other)
    xs = [(camp, ((x + d) % 4) * 2 + core) for d in (1, 2, 3)]
    tms = [(camp, (tm + d) % 8) for d in range(1, 8)]
    zs = [(y * 4 + (z + d) % 4, tm) for d in (1, 2, 3)]
    ys = [(((y + d) % 4) * 4 + z, tm) for d in (1, 2, 3)]
    right, left = xs[0], xs[2]
    my_slots, sib_slots = pl.ds(core * NT, NT), pl.ds(other * NT, NT)
    my_tiles = pl.ds(pl.multiple_of(core * NC, 8), NC)
    sib_tiles = pl.ds(pl.multiple_of(other * NC, 8), NC)

    def lanes(of_core, first, width):
        return pl.ds(pl.multiple_of(of_core * CW + first, 128), width)

    my_lanes = lanes(core, 0, CW)

    def wait_for(like, sem):
        pltpu.make_async_copy(like, like, sem).wait()

    def send(src, dst, ssem, rsem, to):
        return pltpu.make_async_remote_copy(
            src_ref=src, dst_ref=dst, send_sem=ssem, recv_sem=rsem, device_id=to, device_id_type=MESH
        )

    barrier = pltpu.get_barrier_semaphore()
    greet = tms + zs + ys
    for to in greet:
        pl.semaphore_signal(barrier, inc=1, device_id=to, device_id_type=MESH)

    loads = []

    def load(src, dst):
        cp = pltpu.make_async_copy(src, dst, ld.at[len(loads)])
        cp.start()
        loads.append(cp)

    load(p0_hbm, p0_ref)
    load(s0_hbm, rows_ref.at[core, 0])
    load(supply_hbm, rows_ref.at[core, 1])
    for src, dst in (
        (begin_hbm, begin_ref), (span_hbm, span_ref), (limit_hbm, limit_ref),
    ):
        load(src, dst)
    load(elig_hbm.at[:, my_lanes], elig_ref)
    small = len(loads)
    load(value_hbm.at[:, my_lanes], value)
    load(x0_hbm.at[:, :, my_lanes], x0.at[my_slots])
    load(share_hbm.at[:, my_lanes], share)
    load(price_hbm.at[:, my_lanes], price)
    load(r0_hbm.at[:, my_lanes], r0)
    load(rcap_hbm.at[pl.ds(pl.multiple_of(x * QR, 8), QR), my_lanes], rcap)

    for cp in loads[:small]:
        cp.wait()
    for t in range(NT):
        for k in range(2 * NC):
            pka[t, k : k + 1, :] = p0_ref[t : t + 1, k * 128 : (k + 1) * 128]
    tstart[pl.ds(2 * x, 2)] = jnp.zeros((2, NC, 128), jnp.float32)
    tsum[...] = pka[0] + pka[1] + pka[2] + pka[3]
    for t in range(NT):
        pk0[core * NT + t] = pka[t, my_tiles, :]

    begin = begin_ref[my_tiles, :]
    span = span_ref[my_tiles, :]
    limit = limit_ref[my_tiles, :]
    for u in range(NU):
        slot = x * NU + u
        live[u] = ((slot >= begin) & (slot < begin + span)).astype(jnp.float32)

    pl.semaphore_wait(barrier, len(greet))

    for d in (1, 2, 3):
        for c in (0, 1):
            to = (camp, ((x + d) % 4) * 2 + c)
            send(tsum.at[pl.ds(c * NC, NC)], tstart.at[tm], start_s.at[0], start_r.at[0], to).start()
    send(pka.at[:, sib_tiles], pk0.at[my_slots], start_s.at[1], start_r.at[1], sib).start()
    send(rows_ref.at[core], rows_ref.at[core], start_s.at[2], start_r.at[2], sib).start()
    for q in FIRST:
        send(
            x0_hbm.at[:, :, lanes(other, q * 128, 128)], x0.at[my_slots, :, pl.ds(q * 128, 128)], x_s.at[0], x_r.at[q], sib
        ).start()

    def spread_supply(rows):
        s8[...] = rows * -0.5
        table = s8[...]
        for u in range(NU):
            pick = (lax.broadcasted_iota(jnp.int32, (8, 128), 0) == u).astype(jnp.float32)
            sb[u] = lax.dot_general(
                table, pick, (((0,), (0,)), ((), ())), precision=HIGHEST, preferred_element_type=jnp.float32
            )

    for b in range(S // SEG_BLOCK):
        pen[b] = jnp.where(elig_ref[b : b + 1, :] > 0, 0.0, BLOCKED)
    loads[small].wait()

    def value_body(rb, carry):
        rows = pl.ds(pl.multiple_of(rb * 8, 8), 8)
        value[rows, :] = 0.5 * value[rows, :] + pen[rb]
        return carry

    lax.fori_loop(0, S // 8, value_body, 0)
    used[...] = jnp.zeros_like(used)
    for sem in (start_s, start_r):
        wait_for(rows_ref.at[0], sem.at[2])
    s0 = jnp.concatenate([rows_ref[0, 0], rows_ref[1, 0]], axis=0)
    s1[...] = s0
    spread_supply(s0)
    for cp in loads[small + 1 :]:
        cp.wait()

    def masked_total(parts, senders, mine, later):
        total = None
        for m in range(senders):
            keep = (m > mine) if later else (m < mine)
            term = jnp.where(keep, parts(m), 0.0)
            total = term if total is None else total + term
        return total

    def set_zeff(duals, later, rows):
        run = later
        for u in reversed(range(NU)):
            run = run + duals[u]
            zeff[u, rows, :] = jnp.where(live[u, rows, :] > 0.0, -0.5 * run, BLOCKED)

    for sem in (start_s, start_r):
        wait_for(tstart.at[pl.ds(0, 6)], sem.at[0])
        wait_for(pk0.at[pl.ds(0, NT)], sem.at[1])
    set_zeff(
        [pk0[u] for u in range(NU)],
        masked_total(lambda m: tstart[2 * m] + tstart[2 * m + 1], 4, x, True),
        slice(0, NC),
    )

    def comp(it, i):
        cols = pl.ds(i * 128, 128)
        zb = [jnp.broadcast_to(zeff[u, i : i + 1, :], (8, 128)) for u in range(NU)]

        def body(rb, acc):
            rows = pl.ds(pl.multiple_of(rb * 8, 8), 8)
            acc = list(acc)
            sh = share[rows, cols]
            pr = price[rows, cols]
            rd = r0[rows, cols] if it == 0 else r1[rows, cols]
            base = value[rows, cols] - 0.5 * rd
            total = None
            for u in range(NU):
                old = x0[u, rows, cols] if it == 0 else x1[u, rows, cols]
                new = jnp.maximum((old + base) + (sh * sb[u, rows, :] + pr * zb[u]), 0.0)
                bar = (new + new) - old
                acc[u] = acc[u] + pr * bar
                used[u, rows, :] = used[u, rows, :] + sh * bar
                total = bar if total is None else total + bar
                if it == 0:
                    x1[u, rows, cols] = new
                else:
                    x1[u, rows, cols] = (2.0 / 3.0) * bar + (1.0 / 3.0) * x0[u, rows, cols]
            deliv[it, rows, cols] = total
            return tuple(acc)

        zero = jnp.zeros((8, 128), jnp.float32)
        acc = lax.fori_loop(0, S // 8, body, (zero,) * NU, unroll=2)
        for u in range(NU):
            spent[it, u, i : i + 1, :] = jnp.sum(acc[u], axis=0, keepdims=True)

    def part(chip, first, rows):
        return pl.ds(pl.multiple_of(chip * QR + first, 8), rows)

    opposite, after, before = (x + 2) % 4, (x + 1) % 4, (x + 3) % 4

    def two(buf, rows, n=2):
        return buf.at[0, pl.ds(0, n), pl.ds(0, rows), pl.ds(0, 128)]

    def go(it, i, src, dst, rsem, to):
        send(src, dst, sent.at[it], rsem.at[i], to).start()

    def held(it, i):
        if it == 0:
            return r1, pl.ds(i * 128, 128)
        return r_out, lanes(core, i * 128, 128)

    def chunk(it, i):
        if it == 0:
            wait_for(x0.at[pl.ds(0, NT), :, pl.ds(0, 128)], x_r.at[i])
        comp(it, i)

    def hand_over(i, n):
        cols = pl.ds(i * 128, n * 128)
        to = x_out.at[:, :, lanes(core, i * 128, n * 128)]
        send(x1.at[sib_slots, :, cols], to, xo.at[0], xo.at[1], sib).start()
        pltpu.make_async_copy(x1.at[my_slots, :, cols], to, xo.at[2]).start()

    def rs1(it, i):
        cols = pl.ds(i * 128, 128)
        if RS_RING[it][i]:
            go(it, i, deliv.at[it, part(opposite, 0, HR), cols], ring.at[it, 0, :, cols], rs1_r, right)
            go(it, i, deliv.at[it, part(opposite, HR, HR), cols], ring.at[it, 1, :, cols], rs1_r, left)
        else:
            for d, chip, to in ((0, after, xs[0]), (1, before, xs[2]), (2, opposite, xs[1])):
                go(it, i, deliv.at[it, part(chip, 0, QR), cols], from_x.at[it, d, :, cols], rs2_r, to)

    def rs2(it, i):
        cols = pl.ds(i * 128, 128)
        wait_for(two(ring, HR), rs1_r.at[i])
        rows = part(after, 0, HR)
        deliv[it, rows, cols] = deliv[it, rows, cols] + ring[it, 0, :, cols]
        rows = part(before, HR, HR)
        deliv[it, rows, cols] = deliv[it, rows, cols] + ring[it, 1, :, cols]
        go(it, i, deliv.at[it, part(after, 0, QR), cols], from_x.at[it, 0, :, cols], rs2_r, right)
        go(it, i, deliv.at[it, part(before, 0, QR), cols], from_x.at[it, 1, :, cols], rs2_r, left)

    def ag1(it, i):
        cols = pl.ds(i * 128, 128)
        rows = part(x, 0, QR)
        wait_for(two(from_x, QR, 2 if RS_RING[it][i] else 3), rs2_r.at[i])
        total = deliv[it, rows, cols] + from_x[it, 0, :, cols] + from_x[it, 1, :, cols]
        if not RS_RING[it][i]:
            total = total + from_x[it, 2, :, cols]
        start = r0[rows, cols]
        out, where = held(it, i)
        if it == 0:
            r1[rows, cols] = jnp.maximum(start + SIG_REACH * (total - rcap[:, cols]), 0.0)
        else:
            old = r1[rows, cols]
            new = jnp.maximum(old + SIG_REACH * (total - rcap[:, cols]), 0.0)
            r_out[rows, where] = (2.0 / 3.0) * (2.0 * new - old) + (1.0 / 3.0) * start
        piece = out.at[rows, where]
        go(it, i, piece, piece, ag1_r, right)
        go(it, i, piece, piece, ag1_r, left)
        if not AG_RING[it][i]:
            go(it, i, piece, piece, ag1_r, xs[1])

    def ag2(it, i):
        wait_for(two(from_x, QR), ag1_r.at[i])
        out, where = held(it, i)
        piece = out.at[part(before, 0, HR), where]
        go(it, i, piece, piece, ag2_r, right)
        piece = out.at[part(after, HR, HR), where]
        go(it, i, piece, piece, ag2_r, left)

    def gathered(it, i):
        if AG_RING[it][i]:
            wait_for(two(ring, HR), ag2_r.at[i])
        else:
            wait_for(two(from_x, QR, 3), ag1_r.at[i])

    def sibb(it, i):
        gathered(it, i)
        piece = r_out.at[:, lanes(core, i * 128, 128)]
        go(it, i, piece, piece, sibb_r, sib)

    def fin(it, i):
        if it == 0:
            gathered(it, i)
        else:
            wait_for(deliv.at[0, :, pl.ds(0, 128)], sibb_r.at[i])

    def used_z(it):
        total = None
        for u in range(NU):
            term = lax.dot_general(
                jnp.ones((8, 128), jnp.float32), used[u], (((1,), (1,)), ((), ())),
                precision=HIGHEST, preferred_element_type=jnp.float32,
            )
            term = jnp.where(lax.broadcasted_iota(jnp.int32, (8, S), 0) == u, term, 0.0)
            total = term if total is None else total + term
        uz[it, z] = total
        for to in zs:
            send(uz.at[it, z], uz.at[it, z], used_s.at[it, 0], used_r.at[it, 0], to).start()
        if it == 0:
            used[...] = jnp.zeros_like(used)

    def used_y(it):
        for sem in (used_s, used_r):
            wait_for(uz.at[it, pl.ds(0, 3)], sem.at[it, 0])
        uy[it, y] = uz[it, 0] + uz[it, 1] + uz[it, 2] + uz[it, 3]
        for to in ys:
            send(uy.at[it, y], uy.at[it, y], used_s.at[it, 1], used_r.at[it, 1], to).start()

    def used_sib(it):
        for sem in (used_s, used_r):
            wait_for(uy.at[it, pl.ds(0, 3)], sem.at[it, 1])
        us[it, core] = uy[it, 0] + uy[it, 1] + uy[it, 2] + uy[it, 3]
        send(us.at[it, core], us.at[it, core], used_s.at[it, 2], used_r.at[it, 2], sib).start()

    def used_end(it):
        for sem in (used_s, used_r):
            wait_for(us.at[it, 0], sem.at[it, 2])
        total = us[it, 0] + us[it, 1]
        supply = jnp.concatenate([rows_ref[0, 1], rows_ref[1, 1]], axis=0)
        old = s1[...]
        new = jnp.maximum(old + SIG_SUPPLY * (total - supply), 0.0)
        if it == 0:
            s1[...] = new
            spread_supply(new)
        else:
            first = jnp.concatenate([rows_ref[0, 0], rows_ref[1, 0]], axis=0)
            res = (2.0 / 3.0) * (2.0 * new - old) + (1.0 / 3.0) * first
            s_out[...] = jnp.where(core == 0, res[0:NT], res[NT:NU])

    def share_total(e, g, total):
        tots[e, g, x] = total
        for to in xs:
            send(tots.at[e, g, x], tots.at[e, g, x], tot_s.at[e, g], tot_r.at[e, g], to).start()

    def wait_total(e, g, later):
        for sem in (tot_s, tot_r):
            wait_for(tots.at[e, g, pl.ds(0, 3)], sem.at[e, g])
        return masked_total(lambda m: tots[e, g, m], 4, x, later)

    def add_up(terms):
        total = terms[0]
        for term in terms[1:]:
            total = total + term
        return total

    def spend_1(it, g):
        rows = slice(g * GC, (g + 1) * GC)
        share_total(2 * it, g, add_up([spent[it, u, rows] for u in range(NU)]))

    def spend_2(it, g):
        rows = slice(g * GC, (g + 1) * GC)
        run = wait_total(2 * it, g, False)
        fresh = []
        for u in range(NU):
            run = run + spent[it, u, rows]
            old = pk0[u, rows] if it == 0 else pk1[u, rows]
            new = jnp.maximum(old + SIG_SPEND * (run - cap[u, rows]), 0.0)
            if it == 0:
                pk1[u, rows] = new
                fresh.append(new)
            else:
                pres[u, rows] = (2.0 / 3.0) * (2.0 * new - old) + (1.0 / 3.0) * pk0[u, rows]
        if it == 0:
            share_total(1, g, add_up(fresh))

    def spend_3(g):
        rows = slice(g * GC, (g + 1) * GC)
        later = wait_total(1, g, True)
        set_zeff([pk1[u, rows] for u in range(NU)], later, rows)

    def spend_out():
        send(pres.at[sib_slots], pin, pf.at[0], pf.at[1], sib).start()

    def spend_end():
        wait_for(pin, pf.at[0])
        wait_for(pin, pf.at[1])
        for t in range(NT):
            for k in range(NC):
                p_out[t : t + 1, lanes(core, k * 128, 128)] = pres[core * NT + t, k : k + 1, :]
                p_out[t : t + 1, lanes(other, k * 128, 128)] = pin[t, k : k + 1, :]

    def caps():
        for u in range(NU):
            frac = jnp.clip((x * NU + u + 1 - begin).astype(jnp.float32) / span.astype(jnp.float32), 0.0, 1.0)
            cap[u] = limit * frac

    steps = dict(
        comp=chunk, rs1=rs1, rs2=rs2, ag1=ag1, ag2=ag2, sibb=sibb, fin=fin, uz=used_z, uy=used_y, us=used_sib,
        ue=used_end, sp1=spend_1, sp2=spend_2, sp3=spend_3, caps=caps, pf1=spend_out, pf2=spend_end, xo=hand_over,
    )
    for name, *where in ORDER:
        steps[name](*where)
    wait_for(x0.at[pl.ds(0, NT)], x_s.at[0])
    for k in range(3):
        wait_for(x0.at[pl.ds(0, NT)], xo.at[k])
    wait_for(x0.at[pl.ds(0, 3), pl.ds(0, S // 2)], sent.at[0])
    wait_for(x0.at[pl.ds(0, 5), pl.ds(0, S // 2)], sent.at[1])


def write_out(x, s, r, p, x_hbm, s_hbm, r_hbm, p_hbm, sem):
    cps = []

    def store(src, dst):
        cp = pltpu.make_async_copy(src, dst, sem.at[len(cps)])
        cp.start()
        cps.append(cp)

    store(s, s_hbm)
    store(p, p_hbm)
    for t in range(NT):
        store(x.at[t], x_hbm.at[t])
    store(r, r_hbm)
    for cp in cps:
        cp.wait()


def shards(
    primal_start, supply_start, reach_start, spend_start, value, share, price, reach_cap,
    spend_limit, supply, eligible, start_slot, active_span,
):
    f32 = jnp.float32
    vmem = pl.BlockSpec(memory_space=pltpu.VMEM)
    anywhere = pl.BlockSpec(memory_space=pltpu.HBM)
    dma = pltpu.SemaphoreType.DMA
    outs = (
        pltpu.VMEM((NT, S, CD), f32),
        pltpu.VMEM((NT, S), f32),
        pltpu.VMEM((S, CD), f32),
        pltpu.VMEM((NT, CD), f32),
    )
    scratch = [
        pltpu.VMEM((NT, CD), f32),
        pltpu.VMEM((2 * NC, 128), f32),
        pltpu.VMEM((S // SEG_BLOCK, CW), jnp.int32),
        pltpu.VMEM((2 * NC, 128), jnp.int32),
        pltpu.VMEM((2 * NC, 128), jnp.int32),
        pltpu.VMEM((2, 2, NT, S), f32),
        pltpu.VMEM((NU, S, CW), f32),
        pltpu.VMEM((NU, S, CW), f32),
        pltpu.VMEM((S, CW), f32),
        pltpu.VMEM((S, CW), f32),
        pltpu.VMEM((S, CW), f32),
        pltpu.VMEM((S, CW), f32),
        pltpu.VMEM((QR, CW), f32),
        pltpu.VMEM((2, S, CW), f32),
        pltpu.VMEM((2, 2, HR, CW), f32),
        pltpu.VMEM((2, 3, QR, CW), f32),
        pltpu.VMEM((S, CW), f32),
        pltpu.VMEM((S // SEG_BLOCK, 1, CW), f32),
        pltpu.VMEM((NU, S, 128), f32),
        pltpu.VMEM((NU, S), f32),
        pltpu.VMEM((NU, S), f32),
        pltpu.VMEM((NU, S, 128), f32),
        pltpu.VMEM((2, 4, NU, S), f32),
        pltpu.VMEM((2, 4, NU, S), f32),
        pltpu.VMEM((2, 2, NU, S), f32),
        pltpu.VMEM((NT, 2 * NC, 128), f32),
        pltpu.VMEM((NU, NC, 128), f32),
        pltpu.VMEM((NU, NC, 128), f32),
        pltpu.VMEM((NU, NC, 128), f32),
        pltpu.VMEM((NT, NC, 128), f32),
        pltpu.VMEM((NU, NC, 128), f32),
        pltpu.VMEM((NU, NC, 128), f32),
        pltpu.VMEM((NU, NC, 128), f32),
        pltpu.VMEM((2, NU, NC, 128), f32),
        pltpu.VMEM((2 * NC, 128), f32),
        pltpu.VMEM((8, NC, 128), f32),
        pltpu.VMEM((3, NG, 4, GC, 128), f32),
        dma((13,)),
        dma((1,)), dma((NC,)), dma((3,)),
        dma((3,)), dma((3,)),
        dma((2,)),
        dma((NC,)), dma((NC,)), dma((NC,)), dma((NC,)), dma((NC,)),
        dma((3, NG)), dma((3, NG)),
        dma((2, 3)), dma((2, 3)),
        dma((2,)),
    ]
    args = (
        primal_start, supply_start, reach_start, spend_start, value, share, price, reach_cap,
        spend_limit.reshape(2 * NC, 128), supply, eligible,
        start_slot.reshape(2 * NC, 128), active_span.reshape(2 * NC, 128),
    )
    res = pl.pallas_call(
        kernel,
        out_shape=outs,
        in_specs=[anywhere] * 13,
        out_specs=(vmem,) * 4,
        scratch_shapes=scratch,
        compiler_params=pltpu.CompilerParams(
            collective_id=0, has_side_effects=True, vmem_limit_bytes=44 * 2**20
        ),
    )(*[pltpu.with_memory_space_constraint(a, pltpu.HBM) for a in args])
    return tuple(
        pl.pallas_call(
            write_out,
            out_shape=tuple(pltpu.HBM(o.shape, o.dtype) for o in outs),
            in_specs=[vmem] * 4,
            out_specs=(anywhere,) * 4,
            scratch_shapes=[dma((NT + 3,))],
            compiler_params=pltpu.CompilerParams(vmem_limit_bytes=2**20),
        )(*res)
    )


def solution(mesh):
    in_specs = (
        P("tm", None, "camp"), P("tm", None), P(None, "camp"), P("tm", "camp"),
        P(None, "camp"), P(None, "camp"), P(None, "camp"), P(None, "camp"),
        P("camp"), P("tm", None), P(None, "camp"), P("camp"), P("camp"),
    )
    out_specs = (P("tm", None, "camp"), P("tm", None), P(None, "camp"), P("tm", "camp"))
    return jax.shard_map(shards, mesh=mesh, in_specs=in_specs, out_specs=out_specs, check_vma=False)
```

```python
import jax
import jax.numpy as jnp
from jax import lax
from jax.experimental import pallas as pl
from jax.experimental.pallas import tpu as pltpu
from jax.sharding import PartitionSpec as P

S = 192
SEG_BLOCK = 8
SLOTS = 32
CAMPAIGNS = 32768
MESH = pl.DeviceIdType.MESH
HIGHEST = lax.Precision.HIGHEST

NT = 4
NU = 2 * NT
CD = 2048
CW = CD // 2
NC = CW // 128
QR = S // 4
HR = QR // 2
NG = 2
GC = NC // NG
BLOCKED = -1e30

SIG_SUPPLY = 4.0 / CAMPAIGNS
SIG_REACH = 1.0 / (2 * SLOTS)
SIG_SPEND = 1.0 / (S * SLOTS * SLOTS)

RS_RING = ((0, 0, 0, 1, 1, 1, 1, 0), (1, 0, 1, 0, 1, 0, 0, 1))
AG_RING = ((1, 0, 0, 0, 0, 0, 0, 1), (0, 1, 1, 1, 0, 1, 1, 0))
ORDER = (
    ("comp", 0, 0), ("rs1", 0, 0), ("comp", 0, 6), ("comp", 0, 7), ("rs1", 0, 6), ("rs1", 0, 7), ("caps",),
    ("comp", 0, 5), ("comp", 0, 3), ("rs1", 0, 3), ("comp", 0, 4), ("sp1", 0, 1), ("rs1", 0, 4),
    ("rs1", 0, 5), ("comp", 0, 2), ("rs1", 0, 2), ("comp", 0, 1), ("uz", 0), ("rs1", 0, 1), ("rs2", 0, 6),
    ("ag1", 0, 0), ("sp1", 0, 0), ("ag1", 0, 7), ("rs2", 0, 5), ("uy", 0), ("rs2", 0, 4), ("ag1", 0, 2),
    ("rs2", 0, 3), ("sp2", 0, 1), ("ag1", 0, 6), ("ag2", 0, 0), ("sp2", 0, 0), ("ag2", 0, 7), ("ag1", 0, 1),
    ("us", 0), ("ag1", 0, 4), ("fin", 0, 2), ("ag1", 0, 5), ("ag1", 0, 3), ("ue", 0), ("fin", 0, 6),
    ("sp3", 1), ("comp", 1, 6), ("rs1", 1, 6), ("sp3", 0), ("fin", 0, 7), ("fin", 0, 0), ("comp", 1, 2),
    ("comp", 1, 7), ("rs1", 1, 7), ("fin", 0, 1), ("comp", 1, 1), ("rs1", 1, 2), ("rs1", 1, 1), ("fin", 0, 4),
    ("comp", 1, 4), ("rs1", 1, 4), ("comp", 1, 0), ("rs1", 1, 0), ("fin", 0, 5), ("comp", 1, 5),
    ("rs1", 1, 5), ("fin", 0, 3), ("comp", 1, 3), ("rs1", 1, 3), ("xo", 0, 8), ("ag1", 1, 6), ("rs2", 1, 2),
    ("rs2", 1, 4), ("rs2", 1, 7), ("ag1", 1, 1), ("rs2", 1, 0), ("ag1", 1, 5), ("uz", 1), ("sp1", 1, 0), ("sp1", 1, 1), ("ag1", 1, 3),
    ("ag2", 1, 6), ("ag1", 1, 2), ("ag1", 1, 4), ("ag2", 1, 1), ("ag1", 1, 7), ("uy", 1), ("ag1", 1, 0),
    ("ag2", 1, 5), ("ag2", 1, 3), ("sibb", 1, 6), ("ag2", 1, 2), ("sp2", 1, 0), ("sp2", 1, 1), ("pf1",), ("fin", 1, 6),
    ("sibb", 1, 1), ("sibb", 1, 4), ("sibb", 1, 7), ("fin", 1, 1), ("us", 1), ("fin", 1, 4), ("sibb", 1, 0),
    ("sibb", 1, 5), ("sibb", 1, 3), ("sibb", 1, 2), ("fin", 1, 7), ("fin", 1, 0),
    ("fin", 1, 5), ("ue", 1),  ("pf2",), ("fin", 1, 3), ("fin", 1, 2),
)


FIRST = [where[1] for name, *where in ORDER if name == "comp" and where[0] == 0]


def kernel(
    x0_hbm, s0_hbm, r0_hbm, p0_hbm, value_hbm, share_hbm, price_hbm, rcap_hbm,
    limit_hbm, supply_hbm, elig_hbm, begin_hbm, span_hbm,
    x_out, s_out, r_out, p_out,
    p0_ref, limit_ref, elig_ref, begin_ref, span_ref, rows_ref,
    x0, x1, value, share, price, r0, rcap,
    deliv, ring, from_x, r1,
    pen, sb, s8, s1, used, uz, uy, us,
    pka, pk0, pk1, pres, pin, cap, live, zeff, spent, tsum, tstart, tots,
    ld, x_s, x_r, xo, start_s, start_r, sent, rs1_r, rs2_r, ag1_r, ag2_r, sibb_r,
    tot_s, tot_r, used_s, used_r, pf,
):
    camp = lax.axis_index("camp")
    tm = lax.axis_index("tm")
    y, z = camp // 4, camp % 4
    x, core = tm // 2, tm % 2
    other = 1 - core
    sib = (camp, x * 2 + other)
    xs = [(camp, ((x + d) % 4) * 2 + core) for d in (1, 2, 3)]
    tms = [(camp, (tm + d) % 8) for d in range(1, 8)]
    zs = [(y * 4 + (z + d) % 4, tm) for d in (1, 2, 3)]
    ys = [(((y + d) % 4) * 4 + z, tm) for d in (1, 2, 3)]
    right, left = xs[0], xs[2]
    my_slots, sib_slots = pl.ds(core * NT, NT), pl.ds(other * NT, NT)
    my_tiles = pl.ds(pl.multiple_of(core * NC, 8), NC)
    sib_tiles = pl.ds(pl.multiple_of(other * NC, 8), NC)

    def lanes(of_core, first, width):
        return pl.ds(pl.multiple_of(of_core * CW + first, 128), width)

    my_lanes = lanes(core, 0, CW)

    def wait_for(like, sem):
        pltpu.make_async_copy(like, like, sem).wait()

    def send(src, dst, ssem, rsem, to):
        return pltpu.make_async_remote_copy(
            src_ref=src, dst_ref=dst, send_sem=ssem, recv_sem=rsem, device_id=to, device_id_type=MESH
        )

    barrier = pltpu.get_barrier_semaphore()
    greet = tms + zs + ys
    for to in greet:
        pl.semaphore_signal(barrier, inc=1, device_id=to, device_id_type=MESH)

    loads = []

    def load(src, dst):
        cp = pltpu.make_async_copy(src, dst, ld.at[len(loads)])
        cp.start()
        loads.append(cp)

    load(p0_hbm, p0_ref)
    load(s0_hbm, rows_ref.at[core, 0])
    load(supply_hbm, rows_ref.at[core, 1])
    for src, dst in (
        (begin_hbm, begin_ref), (span_hbm, span_ref), (limit_hbm, limit_ref),
    ):
        load(src, dst)
    load(elig_hbm.at[:, my_lanes], elig_ref)
    small = len(loads)
    load(value_hbm.at[:, my_lanes], value)
    load(x0_hbm.at[:, :, my_lanes], x0.at[my_slots])
    load(share_hbm.at[:, my_lanes], share)
    load(price_hbm.at[:, my_lanes], price)
    load(r0_hbm.at[:, my_lanes], r0)
    load(rcap_hbm.at[pl.ds(pl.multiple_of(x * QR, 8), QR), my_lanes], rcap)

    for cp in loads[:small]:
        cp.wait()
    for t in range(NT):
        for k in range(2 * NC):
            pka[t, k : k + 1, :] = p0_ref[t : t + 1, k * 128 : (k + 1) * 128]
    tstart[pl.ds(2 * x, 2)] = jnp.zeros((2, NC, 128), jnp.float32)
    tsum[...] = pka[0] + pka[1] + pka[2] + pka[3]
    for t in range(NT):
        pk0[core * NT + t] = pka[t, my_tiles, :]

    begin = begin_ref[my_tiles, :]
    span = span_ref[my_tiles, :]
    limit = limit_ref[my_tiles, :]
    for u in range(NU):
        slot = x * NU + u
        live[u] = ((slot >= begin) & (slot < begin + span)).astype(jnp.float32)

    pl.semaphore_wait(barrier, len(greet))

    for d in (1, 2, 3):
        for c in (0, 1):
            to = (camp, ((x + d) % 4) * 2 + c)
            send(tsum.at[pl.ds(c * NC, NC)], tstart.at[tm], start_s.at[0], start_r.at[0], to).start()
    send(pka.at[:, sib_tiles], pk0.at[my_slots], start_s.at[1], start_r.at[1], sib).start()
    send(rows_ref.at[core], rows_ref.at[core], start_s.at[2], start_r.at[2], sib).start()
    for q in FIRST:
        send(
            x0_hbm.at[:, :, lanes(other, q * 128, 128)], x0.at[my_slots, :, pl.ds(q * 128, 128)], x_s.at[0], x_r.at[q], sib
        ).start()

    def spread_supply(rows):
        s8[...] = rows * -0.5
        table = s8[...]
        for u in range(NU):
            pick = (lax.broadcasted_iota(jnp.int32, (8, 128), 0) == u).astype(jnp.float32)
            sb[u] = lax.dot_general(
                table, pick, (((0,), (0,)), ((), ())), precision=HIGHEST, preferred_element_type=jnp.float32
            )

    for b in range(S // SEG_BLOCK):
        pen[b] = jnp.where(elig_ref[b : b + 1, :] > 0, 0.0, BLOCKED)
    loads[small].wait()

    def value_body(rb, carry):
        rows = pl.ds(pl.multiple_of(rb * 8, 8), 8)
        value[rows, :] = 0.5 * value[rows, :] + pen[rb]
        return carry

    lax.fori_loop(0, S // 8, value_body, 0)
    used[...] = jnp.zeros_like(used)
    for sem in (start_s, start_r):
        wait_for(rows_ref.at[0], sem.at[2])
    s0 = jnp.concatenate([rows_ref[0, 0], rows_ref[1, 0]], axis=0)
    s1[...] = s0
    spread_supply(s0)
    for cp in loads[small + 1 :]:
        cp.wait()

    def masked_total(parts, senders, mine, later):
        total = None
        for m in range(senders):
            keep = (m > mine) if later else (m < mine)
            term = jnp.where(keep, parts(m), 0.0)
            total = term if total is None else total + term
        return total

    def set_zeff(duals, later, rows):
        run = later
        for u in reversed(range(NU)):
            run = run + duals[u]
            zeff[u, rows, :] = jnp.where(live[u, rows, :] > 0.0, -0.5 * run, BLOCKED)

    for sem in (start_s, start_r):
        wait_for(tstart.at[pl.ds(0, 6)], sem.at[0])
        wait_for(pk0.at[pl.ds(0, NT)], sem.at[1])
    set_zeff(
        [pk0[u] for u in range(NU)],
        masked_total(lambda m: tstart[2 * m] + tstart[2 * m + 1], 4, x, True),
        slice(0, NC),
    )

    def comp(it, i):
        cols = pl.ds(i * 128, 128)
        zb = [jnp.broadcast_to(zeff[u, i : i + 1, :], (8, 128)) for u in range(NU)]

        def body(rb, acc):
            rows = pl.ds(pl.multiple_of(rb * 8, 8), 8)
            acc = list(acc)
            sh = share[rows, cols]
            pr = price[rows, cols]
            rd = r0[rows, cols] if it == 0 else r1[rows, cols]
            base = value[rows, cols] - 0.5 * rd
            total = None
            for u in range(NU):
                old = x0[u, rows, cols] if it == 0 else x1[u, rows, cols]
                new = jnp.maximum((old + base) + (sh * sb[u, rows, :] + pr * zb[u]), 0.0)
                bar = (new + new) - old
                acc[u] = acc[u] + pr * bar
                used[u, rows, :] = used[u, rows, :] + sh * bar
                total = bar if total is None else total + bar
                if it == 0:
                    x1[u, rows, cols] = new
                else:
                    x1[u, rows, cols] = (2.0 / 3.0) * bar + (1.0 / 3.0) * x0[u, rows, cols]
            deliv[it, rows, cols] = total
            return tuple(acc)

        zero = jnp.zeros((8, 128), jnp.float32)
        acc = lax.fori_loop(0, S // 8, body, (zero,) * NU, unroll=4)
        for u in range(NU):
            spent[it, u, i : i + 1, :] = jnp.sum(acc[u], axis=0, keepdims=True)

    def part(chip, first, rows):
        return pl.ds(pl.multiple_of(chip * QR + first, 8), rows)

    opposite, after, before = (x + 2) % 4, (x + 1) % 4, (x + 3) % 4

    def two(buf, rows, n=2):
        return buf.at[0, pl.ds(0, n), pl.ds(0, rows), pl.ds(0, 128)]

    def go(it, i, src, dst, rsem, to):
        send(src, dst, sent.at[it], rsem.at[i], to).start()

    def held(it, i):
        if it == 0:
            return r1, pl.ds(i * 128, 128)
        return r_out, lanes(core, i * 128, 128)

    def chunk(it, i):
        if it == 0:
            wait_for(x0.at[pl.ds(0, NT), :, pl.ds(0, 128)], x_r.at[i])
        comp(it, i)

    def hand_over(i, n):
        cols = pl.ds(i * 128, n * 128)
        to = x_out.at[:, :, lanes(core, i * 128, n * 128)]
        send(x1.at[sib_slots, :, cols], to, xo.at[0], xo.at[1], sib).start()
        pltpu.make_async_copy(x1.at[my_slots, :, cols], to, xo.at[2]).start()

    def rs1(it, i):
        cols = pl.ds(i * 128, 128)
        if RS_RING[it][i]:
            go(it, i, deliv.at[it, part(opposite, 0, HR), cols], ring.at[it, 0, :, cols], rs1_r, right)
            go(it, i, deliv.at[it, part(opposite, HR, HR), cols], ring.at[it, 1, :, cols], rs1_r, left)
        else:
            for d, chip, to in ((0, after, xs[0]), (1, before, xs[2]), (2, opposite, xs[1])):
                go(it, i, deliv.at[it, part(chip, 0, QR), cols], from_x.at[it, d, :, cols], rs2_r, to)

    def rs2(it, i):
        cols = pl.ds(i * 128, 128)
        wait_for(two(ring, HR), rs1_r.at[i])
        rows = part(after, 0, HR)
        deliv[it, rows, cols] = deliv[it, rows, cols] + ring[it, 0, :, cols]
        rows = part(before, HR, HR)
        deliv[it, rows, cols] = deliv[it, rows, cols] + ring[it, 1, :, cols]
        go(it, i, deliv.at[it, part(after, 0, QR), cols], from_x.at[it, 0, :, cols], rs2_r, right)
        go(it, i, deliv.at[it, part(before, 0, QR), cols], from_x.at[it, 1, :, cols], rs2_r, left)

    def ag1(it, i):
        cols = pl.ds(i * 128, 128)
        rows = part(x, 0, QR)
        wait_for(two(from_x, QR, 2 if RS_RING[it][i] else 3), rs2_r.at[i])
        total = deliv[it, rows, cols] + from_x[it, 0, :, cols] + from_x[it, 1, :, cols]
        if not RS_RING[it][i]:
            total = total + from_x[it, 2, :, cols]
        start = r0[rows, cols]
        out, where = held(it, i)
        if it == 0:
            r1[rows, cols] = jnp.maximum(start + SIG_REACH * (total - rcap[:, cols]), 0.0)
        else:
            old = r1[rows, cols]
            new = jnp.maximum(old + SIG_REACH * (total - rcap[:, cols]), 0.0)
            r_out[rows, where] = (2.0 / 3.0) * (2.0 * new - old) + (1.0 / 3.0) * start
        piece = out.at[rows, where]
        go(it, i, piece, piece, ag1_r, right)
        go(it, i, piece, piece, ag1_r, left)
        if not AG_RING[it][i]:
            go(it, i, piece, piece, ag1_r, xs[1])

    def ag2(it, i):
        wait_for(two(from_x, QR), ag1_r.at[i])
        out, where = held(it, i)
        piece = out.at[part(before, 0, HR), where]
        go(it, i, piece, piece, ag2_r, right)
        piece = out.at[part(after, HR, HR), where]
        go(it, i, piece, piece, ag2_r, left)

    def gathered(it, i):
        if AG_RING[it][i]:
            wait_for(two(ring, HR), ag2_r.at[i])
        else:
            wait_for(two(from_x, QR, 3), ag1_r.at[i])

    def sibb(it, i):
        gathered(it, i)
        piece = r_out.at[:, lanes(core, i * 128, 128)]
        go(it, i, piece, piece, sibb_r, sib)

    def fin(it, i):
        if it == 0:
            gathered(it, i)
        else:
            wait_for(deliv.at[0, :, pl.ds(0, 128)], sibb_r.at[i])

    def used_z(it):
        total = None
        for u in range(NU):
            term = lax.dot_general(
                jnp.ones((8, 128), jnp.float32), used[u], (((1,), (1,)), ((), ())),
                precision=HIGHEST, preferred_element_type=jnp.float32,
            )
            term = jnp.where(lax.broadcasted_iota(jnp.int32, (8, S), 0) == u, term, 0.0)
            total = term if total is None else total + term
        uz[it, z] = total
        for to in zs:
            send(uz.at[it, z], uz.at[it, z], used_s.at[it, 0], used_r.at[it, 0], to).start()
        if it == 0:
            used[...] = jnp.zeros_like(used)

    def used_y(it):
        for sem in (used_s, used_r):
            wait_for(uz.at[it, pl.ds(0, 3)], sem.at[it, 0])
        uy[it, y] = uz[it, 0] + uz[it, 1] + uz[it, 2] + uz[it, 3]
        for to in ys:
            send(uy.at[it, y], uy.at[it, y], used_s.at[it, 1], used_r.at[it, 1], to).start()

    def used_sib(it):
        for sem in (used_s, used_r):
            wait_for(uy.at[it, pl.ds(0, 3)], sem.at[it, 1])
        us[it, core] = uy[it, 0] + uy[it, 1] + uy[it, 2] + uy[it, 3]
        send(us.at[it, core], us.at[it, core], used_s.at[it, 2], used_r.at[it, 2], sib).start()

    def used_end(it):
        for sem in (used_s, used_r):
            wait_for(us.at[it, 0], sem.at[it, 2])
        total = us[it, 0] + us[it, 1]
        supply = jnp.concatenate([rows_ref[0, 1], rows_ref[1, 1]], axis=0)
        old = s1[...]
        new = jnp.maximum(old + SIG_SUPPLY * (total - supply), 0.0)
        if it == 0:
            s1[...] = new
            spread_supply(new)
        else:
            first = jnp.concatenate([rows_ref[0, 0], rows_ref[1, 0]], axis=0)
            res = (2.0 / 3.0) * (2.0 * new - old) + (1.0 / 3.0) * first
            s_out[...] = jnp.where(core == 0, res[0:NT], res[NT:NU])

    def share_total(e, g, total):
        tots[e, g, x] = total
        for to in xs:
            send(tots.at[e, g, x], tots.at[e, g, x], tot_s.at[e, g], tot_r.at[e, g], to).start()

    def wait_total(e, g, later):
        for sem in (tot_s, tot_r):
            wait_for(tots.at[e, g, pl.ds(0, 3)], sem.at[e, g])
        return masked_total(lambda m: tots[e, g, m], 4, x, later)

    def add_up(terms):
        total = terms[0]
        for term in terms[1:]:
            total = total + term
        return total

    def spend_1(it, g):
        rows = slice(g * GC, (g + 1) * GC)
        share_total(2 * it, g, add_up([spent[it, u, rows] for u in range(NU)]))

    def spend_2(it, g):
        rows = slice(g * GC, (g + 1) * GC)
        run = wait_total(2 * it, g, False)
        fresh = []
        for u in range(NU):
            run = run + spent[it, u, rows]
            old = pk0[u, rows] if it == 0 else pk1[u, rows]
            new = jnp.maximum(old + SIG_SPEND * (run - cap[u, rows]), 0.0)
            if it == 0:
                pk1[u, rows] = new
                fresh.append(new)
            else:
                pres[u, rows] = (2.0 / 3.0) * (2.0 * new - old) + (1.0 / 3.0) * pk0[u, rows]
        if it == 0:
            share_total(1, g, add_up(fresh))

    def spend_3(g):
        rows = slice(g * GC, (g + 1) * GC)
        later = wait_total(1, g, True)
        set_zeff([pk1[u, rows] for u in range(NU)], later, rows)

    def spend_out():
        send(pres.at[sib_slots], pin, pf.at[0], pf.at[1], sib).start()

    def spend_end():
        wait_for(pin, pf.at[0])
        wait_for(pin, pf.at[1])
        for t in range(NT):
            for k in range(NC):
                p_out[t : t + 1, lanes(core, k * 128, 128)] = pres[core * NT + t, k : k + 1, :]
                p_out[t : t + 1, lanes(other, k * 128, 128)] = pin[t, k : k + 1, :]

    def caps():
        for u in range(NU):
            frac = jnp.clip((x * NU + u + 1 - begin).astype(jnp.float32) / span.astype(jnp.float32), 0.0, 1.0)
            cap[u] = limit * frac

    steps = dict(
        comp=chunk, rs1=rs1, rs2=rs2, ag1=ag1, ag2=ag2, sibb=sibb, fin=fin, uz=used_z, uy=used_y, us=used_sib,
        ue=used_end, sp1=spend_1, sp2=spend_2, sp3=spend_3, caps=caps, pf1=spend_out, pf2=spend_end, xo=hand_over,
    )
    for name, *where in ORDER:
        steps[name](*where)
    wait_for(x0.at[pl.ds(0, NT)], x_s.at[0])
    for k in range(3):
        wait_for(x0.at[pl.ds(0, NT)], xo.at[k])
    wait_for(x0.at[pl.ds(0, 3), pl.ds(0, S // 2)], sent.at[0])
    wait_for(x0.at[pl.ds(0, 5), pl.ds(0, S // 2)], sent.at[1])


def write_out(x, s, r, p, x_hbm, s_hbm, r_hbm, p_hbm, sem):
    cps = []

    def store(src, dst):
        cp = pltpu.make_async_copy(src, dst, sem.at[len(cps)])
        cp.start()
        cps.append(cp)

    store(s, s_hbm)
    store(p, p_hbm)
    for t in range(NT):
        store(x.at[t], x_hbm.at[t])
    store(r, r_hbm)
    for cp in cps:
        cp.wait()


def shards(
    primal_start, supply_start, reach_start, spend_start, value, share, price, reach_cap,
    spend_limit, supply, eligible, start_slot, active_span,
):
    f32 = jnp.float32
    vmem = pl.BlockSpec(memory_space=pltpu.VMEM)
    anywhere = pl.BlockSpec(memory_space=pltpu.HBM)
    dma = pltpu.SemaphoreType.DMA
    outs = (
        pltpu.VMEM((NT, S, CD), f32),
        pltpu.VMEM((NT, S), f32),
        pltpu.VMEM((S, CD), f32),
        pltpu.VMEM((NT, CD), f32),
    )
    scratch = [
        pltpu.VMEM((NT, CD), f32),
        pltpu.VMEM((2 * NC, 128), f32),
        pltpu.VMEM((S // SEG_BLOCK, CW), jnp.int32),
        pltpu.VMEM((2 * NC, 128), jnp.int32),
        pltpu.VMEM((2 * NC, 128), jnp.int32),
        pltpu.VMEM((2, 2, NT, S), f32),
        pltpu.VMEM((NU, S, CW), f32),
        pltpu.VMEM((NU, S, CW), f32),
        pltpu.VMEM((S, CW), f32),
        pltpu.VMEM((S, CW), f32),
        pltpu.VMEM((S, CW), f32),
        pltpu.VMEM((S, CW), f32),
        pltpu.VMEM((QR, CW), f32),
        pltpu.VMEM((2, S, CW), f32),
        pltpu.VMEM((2, 2, HR, CW), f32),
        pltpu.VMEM((2, 3, QR, CW), f32),
        pltpu.VMEM((S, CW), f32),
        pltpu.VMEM((S // SEG_BLOCK, 1, CW), f32),
        pltpu.VMEM((NU, S, 128), f32),
        pltpu.VMEM((NU, S), f32),
        pltpu.VMEM((NU, S), f32),
        pltpu.VMEM((NU, S, 128), f32),
        pltpu.VMEM((2, 4, NU, S), f32),
        pltpu.VMEM((2, 4, NU, S), f32),
        pltpu.VMEM((2, 2, NU, S), f32),
        pltpu.VMEM((NT, 2 * NC, 128), f32),
        pltpu.VMEM((NU, NC, 128), f32),
        pltpu.VMEM((NU, NC, 128), f32),
        pltpu.VMEM((NU, NC, 128), f32),
        pltpu.VMEM((NT, NC, 128), f32),
        pltpu.VMEM((NU, NC, 128), f32),
        pltpu.VMEM((NU, NC, 128), f32),
        pltpu.VMEM((NU, NC, 128), f32),
        pltpu.VMEM((2, NU, NC, 128), f32),
        pltpu.VMEM((2 * NC, 128), f32),
        pltpu.VMEM((8, NC, 128), f32),
        pltpu.VMEM((3, NG, 4, GC, 128), f32),
        dma((13,)),
        dma((1,)), dma((NC,)), dma((3,)),
        dma((3,)), dma((3,)),
        dma((2,)),
        dma((NC,)), dma((NC,)), dma((NC,)), dma((NC,)), dma((NC,)),
        dma((3, NG)), dma((3, NG)),
        dma((2, 3)), dma((2, 3)),
        dma((2,)),
    ]
    args = (
        primal_start, supply_start, reach_start, spend_start, value, share, price, reach_cap,
        spend_limit.reshape(2 * NC, 128), supply, eligible,
        start_slot.reshape(2 * NC, 128), active_span.reshape(2 * NC, 128),
    )
    res = pl.pallas_call(
        kernel,
        out_shape=outs,
        in_specs=[anywhere] * 13,
        out_specs=(vmem,) * 4,
        scratch_shapes=scratch,
        compiler_params=pltpu.CompilerParams(
            collective_id=0, has_side_effects=True, vmem_limit_bytes=44 * 2**20
        ),
    )(*[pltpu.with_memory_space_constraint(a, pltpu.HBM) for a in args])
    return tuple(
        pl.pallas_call(
            write_out,
            out_shape=tuple(pltpu.HBM(o.shape, o.dtype) for o in outs),
            in_specs=[vmem] * 4,
            out_specs=(anywhere,) * 4,
            scratch_shapes=[dma((NT + 3,))],
            compiler_params=pltpu.CompilerParams(vmem_limit_bytes=2**20),
        )(*res)
    )


def solution(mesh):
    in_specs = (
        P("tm", None, "camp"), P("tm", None), P(None, "camp"), P("tm", "camp"),
        P(None, "camp"), P(None, "camp"), P(None, "camp"), P(None, "camp"),
        P("camp"), P("tm", None), P(None, "camp"), P("camp"), P("camp"),
    )
    out_specs = (P("tm", None, "camp"), P("tm", None), P(None, "camp"), P("tm", "camp"))
    return jax.shard_map(shards, mesh=mesh, in_specs=in_specs, out_specs=out_specs, check_vma=False)
```
